768 devices in a mesh: row: 96 (over x, z, core), col: 8 (over y).
Axes of the slice: x: 4, y: 8, z: 12, core: 2. Of those that a mesh axis runs over, the one named last changes fastest.
Arguments:
- values: float32 [12288, 1024], P('row', 'col'), may hold values from -0.66 to 0.66
- column_ids: int32 [192, 16], P('row', 'col'), may hold values from 0 to 23, as said below
- counts: int32 [192, 8], P('row', 'col'), may hold values from 1 to 2
- keep_pattern: int32 [192, 192], P('row', 'col'), may hold values 0 or 1
Outputs:
- square: float32 [12288, 12288], P('row', 'col')
- purified: float32 [12288, 12288], P('row', 'col')
The draws below stay inside these ranges and needn't reach their ends.
Inputs may be any that keep to these rules, and one draw needn't show every extreme that they name: `column_ids`: within one block row and panel the live slots name distinct block columns.
All inputs are finite; a program needn't handle non-finite values. No bound on the sum of `keep_pattern` on one device may be relied on, other than what follows from the above.
Results may differ from the reference program's by a relative error of at most 0.00008.
Values sent between devices are 32-bit elements; how exact they have to be, the bound alone decides.
A program may use at most 64 MiB of HBM per device.

```python
import jax
import jax.numpy as jnp
from jax import lax

BLK = 64
KS = 2
NB = 192
CB = 24
N_COL = 8


def draw_column_ids(key, part):
    key = jax.random.fold_in(key, 11)
    scores = jax.random.randint(key, (NB, N_COL, CB), 0, 1 << 20) * CB + jnp.arange(CB, dtype=jnp.int32)
    order = jnp.argsort(scores, axis=-1, stable=True).astype(jnp.int32)
    return order[:, :, :KS].reshape(NB, N_COL * KS)


def draw_counts(key, part):
    key = jax.random.fold_in(key, 23)
    first, second = jax.random.split(key)
    drawn = jax.random.randint(first, (NB, N_COL), 1, KS + 1)
    where_full = jax.random.randint(second, (), 0, NB * N_COL)
    flat = jnp.where(jnp.arange(NB * N_COL, dtype=jnp.int32) == where_full, KS, drawn.reshape(-1))
    return flat.reshape(NB, N_COL).astype(jnp.int32)


def touch_ends(values, stream_key, smallest, top_value):
    longest = values.shape.index(max(values.shape))
    spots = []
    for shift in (0, 1):
        where = [jax.random.randint(jax.random.fold_in(stream_key, axis), (), 0, length) for axis, length in enumerate(values.shape)]
        where[longest] = (where[longest] + shift) % values.shape[longest]
        spots.append(tuple(where))
    return values.at[spots[0]].set(smallest).at[spots[1]].set(top_value)


def levels(own_key, shape, shards, smallest, high):
    gain = 1.0
    for position, blocks in shards:
        draws = jax.random.uniform(jax.random.fold_in(jax.random.fold_in(own_key, 6), position), (blocks,), jnp.float32, smallest / len(shards), high / len(shards))
        gain = gain * jnp.repeat(jnp.exp(draws), shape[position] // blocks).reshape((-1,) + (1,) * (len(shape) - 1 - position))
    return gain


def scatter_about(key, dims, deviation, reach, cuts=(), held_as=jnp.bfloat16):
    array = jax.random.normal(key, dims, jnp.float32) * deviation
    if len(cuts) > 0:
        array = levels(key, dims, cuts, -0.22, 0.18) * array
    return jnp.clip(array, min=-reach, max=reach).astype(held_as)


def setup_inputs(seed: int = 0) -> dict:
    key_list = jax.random.split(jax.random.key(seed), 5)
    values = scatter_about(key_list[0], (NB * BLK, N_COL * KS * BLK), 0.11, 0.66, ((0, 96), (1, 8)), jnp.float32)
    column_ids = draw_column_ids(jax.random.fold_in(key_list[4], 71), 0)
    counts = draw_counts(jax.random.fold_in(key_list[4], 71), 0)
    keep_pattern = touch_ends((jax.random.randint(key_list[3], (NB, NB), 0, 4) < 3).astype(jnp.int32), jax.random.fold_in(key_list[3], 1), 0, 1)
    return {"values": values, "column_ids": column_ids, "counts": counts, "keep_pattern": keep_pattern}


def reference(values, column_ids, counts, keep_pattern):
    nb = column_ids.shape[0]
    ncol = counts.shape[1]
    slots = column_ids.shape[1] // ncol
    cb = nb // ncol
    tiles = values.reshape(nb, BLK, ncol, slots, BLK)
    local_ids = column_ids.reshape(nb, ncol, slots)
    global_ids = local_ids + (jnp.arange(ncol, dtype=jnp.int32) * cb)[None, :, None]
    live = jnp.arange(slots, dtype=jnp.int32)[None, None, :] < counts[:, :, None]
    onehot = ((global_ids[..., None] == jnp.arange(nb, dtype=jnp.int32)) & live[..., None]).astype(jnp.float32)
    dense = jnp.einsum("ipsk,iapsb->iakb", onehot, tiles, precision=lax.Precision.HIGHEST)
    dense = dense.reshape(nb * BLK, nb * BLK)
    keep = jnp.repeat(jnp.repeat(keep_pattern.astype(jnp.float32), BLK, axis=0), BLK, axis=1)
    square = keep * jnp.dot(dense, dense, precision=lax.Precision.HIGHEST, preferred_element_type=jnp.float32)
    cube = keep * jnp.dot(square, dense, precision=lax.Precision.HIGHEST, preferred_element_type=jnp.float32)
    return square, 3.0 * square - 2.0 * cube
```

```python
import functools

import jax
import jax.numpy as jnp
from jax import lax
from jax.experimental import pallas as pl
from jax.experimental.pallas import tpu as pltpu
from jax.sharding import PartitionSpec as P

MESH = pl.DeviceIdType.MESH
NX, NZ, NY = 4, 12, 8
BLK = 64
TWO = 2 * BLK
NP = 4
CP = BLK // NP
EXTRA = 8
F32, BF16, I32 = jnp.float32, jnp.bfloat16, jnp.int32


def place():
    row, col = lax.axis_index("row"), lax.axis_index("col")
    return row // (2 * NZ), (row // 2) % NZ, row % 2, col


def to(x, z, core, y):
    return ((x * NZ + z) * 2 + core, y)


def greet(partners):
    barrier = pltpu.get_barrier_semaphore()
    for partner in partners:
        pl.semaphore_signal(barrier, inc=1, device_id=partner, device_id_type=MESH)
    pl.semaphore_wait(barrier, len(partners))


def copy(ref, send, recv, target):
    return pltpu.make_async_remote_copy(
        src_ref=ref, dst_ref=ref, send_sem=send, recv_sem=recv, device_id=target, device_id_type=MESH
    )


def split(a):
    high = a.astype(BF16)
    return high, (a - high.astype(F32)).astype(BF16)


def dot(a, b):
    return jnp.dot(a, b, preferred_element_type=F32)


def gather_panel(
    ids, counts, tile, panel, row, xs, xr, zs, zr, ss, sr, ys, yr
):
    x, z, core, y = place()
    west, east = (z + NZ - 1) % NZ, (z + 1) % NZ
    south, north = (y + NY - 1) % NY, (y + 1) % NY
    greet(
        [to((x + d) % NX, z, core, y) for d in range(1, NX)]
        + [to(x, west, core, y), to(x, east, core, y), to(x, z, 1 - core, y)]
        + [to(x, z, core, south), to(x, z, core, north)]
    )
    at_row = lax.broadcasted_iota(I32, (TWO, TWO), 0)
    at_lane = lax.broadcasted_iota(I32, (TWO, TWO), 1)
    live = jnp.where(at_row < BLK, counts[0, 0], counts[1, 0])
    held = jnp.where(at_lane // BLK < live, tile[...], 0.0).T
    lane = lax.broadcasted_iota(I32, (EXTRA, TWO), 1)
    tags = jnp.where(
        lane == 0, ids[0, 0], jnp.where(lane == 1, ids[0, 1], jnp.where(lane == 2, ids[1, 0], ids[1, 1]))
    ).astype(F32)
    row[y, :TWO] = held
    row[y, TWO:] = tags
    for h in range(NP):
        for s in range(2):
            at = (h * 2 + s) * CP
            panel[z, core, x, at : at + CP] = held[s * BLK + h * CP : s * BLK + (h + 1) * CP]
    panel[z, core, x, TWO:] = tags

    started = []

    def start(c):
        c.start()
        started.append(c)

    def y_copy(way, hop):
        slot = (y - hop) % NY if way == 0 else (y + hop) % NY
        return copy(row.at[slot], ys.at[way, hop], yr.at[way, hop], to(x, z, core, north if way == 0 else south))

    def z_copy(way, hop):
        slot = (z + NZ - hop) % NZ if way == 0 else (z + hop) % NZ
        return copy(panel.at[slot, core], zs.at[way, hop], zr.at[way, hop], to(x, east if way == 0 else west, core, y))

    def sibling(slot, n):
        return copy(panel.at[slot, core], ss.at[n], sr.at[n], to(x, z, 1 - core, y))

    y_hops, z_hops = (NY // 2, NY - 1 - NY // 2), (NZ // 2, NZ - 1 - NZ // 2)
    xc = []
    for d in range(1, NX):
        xc.append(copy(panel.at[z, core, x], xs.at[d - 1], xr.at[d - 1], to((x + d) % NX, z, core, y)))
        start(xc[-1])
    for way in range(2):
        if y_hops[way]:
            start(y_copy(way, 0))
    for c in xc:
        c.wait_recv()
    for way in range(2):
        if z_hops[way]:
            start(z_copy(way, 0))
    start(sibling(z, 0))
    for hop in range(1, max(NZ, NY) // 2 + 1):
        for way in range(2):
            if hop <= z_hops[way]:
                z_copy(way, hop - 1).wait_recv()
                if hop < z_hops[way]:
                    start(z_copy(way, hop))
                slot = (z + NZ - hop) % NZ if way == 0 else (z + hop) % NZ
                start(sibling(slot, hop if way == 0 else NZ - hop))
        for way in range(2):
            if hop <= y_hops[way]:
                y_copy(way, hop - 1).wait_recv()
                if hop < y_hops[way]:
                    start(y_copy(way, hop))
    for n in range(NZ):
        sibling(z, n).wait_recv()
    for c in started:
        c.wait_send()


def offsets(per):
    sizes = (("slot", 4 * NY), ("half", 4 * NY), ("prev1", 8 * NY), ("last1", per), ("prev2", NY * 2 * per), ("last2", NY * per))
    out, at = {}, 0
    for name, size in sizes:
        out[name] = at
        at += size
    return out


def purify(
    per, table, panel, row, keep, keep_out, square, purified, parts, first, second, total, ys, yr
):
    x, z, core, y = place()
    south, north = (y + NY - 1) % NY, (y + 1) % NY
    greet([to(x, z, core, south), to(x, z, core, north)])
    at = offsets(per)
    near = NY // 2

    def hops(h):
        longer, shorter = near, NY - 1 - near
        return (longer, shorter) if h % 2 == 0 else (shorter, longer)

    def y_copy(h, way, hop):
        slot = (y + NY - hop) % NY if way == 0 else (y + hop) % NY
        return copy(
            parts[h].at[slot], ys.at[h, way, hop], yr.at[h, way, hop], to(x, z, core, north if way == 0 else south)
        )

    started = []

    def start(c):
        c.start()
        started.append(c)

    first[8 * NY] = jnp.zeros((CP, TWO), F32)
    second[2 * per] = jnp.zeros((BLK, TWO), F32)
    lanes = lax.broadcasted_iota(I32, (2 * CP, TWO), 1) // BLK
    side = lax.broadcasted_iota(I32, (CP, TWO), 1) // BLK

    def first_part(h):
        def one_panel(q, _):
            high_w, low_w = split(row[q, :TWO])
            wide = jnp.concatenate([high_w, low_w], axis=1)
            stack = []
            for n in range(4):
                e = q * 4 + n
                block = panel[table[at["slot"] + e], 2 * CP * h : 2 * CP * (h + 1), :]
                block = jnp.where(table[at["half"] + e] == n % 2, block, pltpu.roll(block, BLK, 1))
                stack.append(jnp.where(lanes == n % 2, block, 0.0))
            high, low = split(jnp.concatenate(stack, axis=0))
            both = dot(high, wide)
            made = both[:, :TWO] + both[:, TWO:] + dot(low, high_w)
            for n in range(8):
                e = q * 8 + n
                term = jnp.where(side == n // 4, made[n * CP : (n + 1) * CP], 0.0)
                first[e] = term + first[table[at["prev1"] + e]]
            return 0

        lax.fori_loop(0, NY, one_panel, 0)

        def one_column(j, _):
            parts[h][y, j] = first[table[at["last1"] + j]] * keep[j]
            return 0

        lax.fori_loop(0, per, one_column, 0)

    def second_piece(q, fresh):
        def one_device(d, _):
            device = q * (per // 2) + d
            slot = ((device // 2) % NZ * 2 + device % 2) * NX + device // (2 * NZ)
            high, low = split(panel[slot, :TWO, :])
            halves = [
                split(jnp.concatenate([parts[h][q, d * 2 + r] for h in range(NP)], axis=0)) for r in range(2)
            ]
            none = jnp.zeros((BLK, TWO), BF16)
            high_w, low_w = (
                jnp.concatenate(
                    [
                        jnp.concatenate([halves[0][v], none], axis=1),
                        jnp.concatenate([none, halves[1][v]], axis=1),
                    ],
                    axis=0,
                )
                for v in range(2)
            )
            made = dot(jnp.concatenate([high, low], axis=1), jnp.concatenate([high_w, high_w], axis=0))
            made = made + dot(high, low_w)
            for r in range(2):
                for s in range(2):
                    e = d * 4 + r * 2 + s
                    before = second[table[at["prev2"] + q * 2 * per + e]]
                    term = jnp.concatenate(
                        [
                            made[(h * 2 + s) * CP : (h * 2 + s + 1) * CP, r * TWO : (r + 1) * TWO]
                            for h in range(NP)
                        ],
                        axis=0,
                    )
                    second[e] = term + before
            return 0

        lax.fori_loop(0, per // 2, one_device, 0)

        def one_column(j, _):
            new = second[table[at["last2"] + q * per + j]]
            total[j] = new if fresh else total[j] + new
            return 0

        lax.fori_loop(0, per, one_column, 0)

    for h in range(NP):
        first_part(h)
        for way in range(2):
            if hops(h)[way]:
                start(y_copy(h, way, 0))
    second_piece(y, True)

    def own(pair):
        return jnp.concatenate([parts[h][y, pair * 2 + b] for b in range(2) for h in range(NP)], axis=0)

    for pair in range(per // 2):
        square[:, pair * TWO : (pair + 1) * TWO] = own(pair).T

    for hop in range(1, near + 1):
        for h in range(NP):
            for way in range(2):
                if hop <= hops(h)[way]:
                    y_copy(h, way, hop - 1).wait_recv()
                    if hop < hops(h)[way]:
                        start(y_copy(h, way, hop))
        second_piece((y + NY - hop) % NY, False)
        if 2 * hop < NY:
            second_piece((y + hop) % NY, False)
    for pair in range(per // 2):
        cube = jnp.concatenate([total[pair * 2 + b] * keep_out[pair * 2 + b] for b in range(2)], axis=0)
        purified[:, pair * TWO : (pair + 1) * TWO] = (3.0 * own(pair) - 2.0 * cube).T
    for c in started:
        c.wait_send()


def chain(ids, per, none):
    n = ids.shape[-1]
    spot = jnp.arange(n, dtype=I32)
    same = (ids[..., :, None] == ids[..., None, :]) & (spot[None, :] < spot[:, None])
    prev = jnp.max(jnp.where(same, spot, -1), axis=-1)
    here = ids[..., None, :] == jnp.arange(per, dtype=I32)[:, None]
    last = jnp.max(jnp.where(here, spot, -1), axis=-1)
    return jnp.where(prev < 0, none, prev), jnp.where(last < 0, none, last)


def local(values, column_ids, counts, keep_pattern):
    per = keep_pattern.shape[1]
    nb = 2 * lax.axis_size("row")
    vmem, smem = pl.BlockSpec(memory_space=pltpu.VMEM), pl.BlockSpec(memory_space=pltpu.SMEM)
    rows = TWO + EXTRA
    dma = pltpu.SemaphoreType.DMA
    panel, row = pl.pallas_call(
        gather_panel,
        out_shape=(
            jax.ShapeDtypeStruct((NZ, 2, NX, rows, TWO), F32),
            jax.ShapeDtypeStruct((NY, rows, TWO), F32),
        ),
        in_specs=[smem, smem, vmem],
        out_specs=(vmem, vmem),
        scratch_shapes=[
            dma((NX - 1,)), dma((NX - 1,)),
            dma((2, NZ)), dma((2, NZ)),
            dma((NZ,)), dma((NZ,)),
            dma((2, NY)), dma((2, NY)),
        ],
        compiler_params=pltpu.CompilerParams(
            collective_id=0, has_side_effects=True, vmem_limit_bytes=24 << 20
        ),
        name="gather_panel",
    )(column_ids, counts, values)

    tags = panel[:, :, :, TWO, :4].astype(I32)
    ids = tags.transpose(2, 0, 1, 3).reshape(nb, 2)
    mine = row[:, TWO, :4].astype(I32)
    block = (mine + jnp.arange(NY, dtype=I32)[:, None] * per).reshape(-1)
    device = block // 2
    slot = ((device // 2) % NZ * 2 + device % 2) * NX + device // (2 * NZ)
    onto = jnp.sum(
        jnp.where((block[:, None] == jnp.arange(nb, dtype=I32)[None, :])[:, :, None], ids[None], 0), axis=1
    )
    prev1, last1 = chain(onto.reshape(-1), per, 8 * NY)
    prev2, last2 = chain(ids.reshape(NY, 2 * per), per, 2 * per)
    table = jnp.concatenate(
        [slot, block % 2, prev1, last1, prev2.reshape(-1), last2.reshape(-1)]
    ).astype(I32)
    keep = jnp.repeat(keep_pattern.astype(F32).T, BLK, axis=1)[:, None, :]

    def body(table, panel, row, keep, square, purified, *rest):
        parts = rest[:NP]
        purify(per, table, panel, row, keep, keep, square, purified, parts, *rest[NP:])

    square, purified = pl.pallas_call(
        body,
        out_shape=(
            jax.ShapeDtypeStruct((TWO, per * BLK), F32),
            jax.ShapeDtypeStruct((TWO, per * BLK), F32),
        ),
        in_specs=[smem, vmem, vmem, vmem],
        out_specs=(vmem, vmem),
        scratch_shapes=[pltpu.VMEM((NY, per, CP, TWO), F32) for _ in range(NP)]
        + [
            pltpu.VMEM((8 * NY + 1, CP, TWO), F32),
            pltpu.VMEM((2 * per + 1, BLK, TWO), F32),
            pltpu.VMEM((per, BLK, TWO), F32),
            dma((NP, 2, NY)), dma((NP, 2, NY)),
        ],
        compiler_params=pltpu.CompilerParams(
            collective_id=1, has_side_effects=True, vmem_limit_bytes=48 << 20
        ),
        name="purify",
    )(table, panel.reshape(NZ * 2 * NX, rows, TWO), row, keep)
    return square, purified


def solution(mesh):
    return jax.shard_map(
        local,
        mesh=mesh,
        in_specs=(P("row", "col"), P("row", "col"), P("row", "col"), P("row", "col")),
        out_specs=(P("row", "col"), P("row", "col")),
        check_vma=False,
    )
```

```python
import jax
import jax.numpy as jnp
from jax import lax
from jax.experimental import pallas as pl
from jax.experimental.pallas import tpu as pltpu
from jax.sharding import PartitionSpec as P

MESH = pl.DeviceIdType.MESH
NX, NZ, NY = 4, 12, 8
BLK = 64
TWO = 2 * BLK
NP = 4
AHEAD = 2
CP = BLK // NP
EXTRA = 8
F32, BF16, I32 = jnp.float32, jnp.bfloat16, jnp.int32


def place():
    row, col = lax.axis_index("row"), lax.axis_index("col")
    return row // (2 * NZ), (row // 2) % NZ, row % 2, col


def to(x, z, core, y):
    return ((x * NZ + z) * 2 + core, y)


def greet(partners):
    barrier = pltpu.get_barrier_semaphore()
    for partner in partners:
        pl.semaphore_signal(barrier, inc=1, device_id=partner, device_id_type=MESH)
    pl.semaphore_wait(barrier, len(partners))


def send(src, dst, sems, at, target):
    return pltpu.make_async_remote_copy(
        src_ref=src, dst_ref=dst, send_sem=sems[0].at[at], recv_sem=sems[1].at[at], device_id=target, device_id_type=MESH
    )


def split(a):
    high = a.astype(BF16)
    return high, (a - high.astype(F32)).astype(BF16)


def dot(a, b):
    return jnp.dot(a, b, preferred_element_type=F32)


def part_rows(h):
    return 2 * CP + (EXTRA if h == 0 else 0)


def iota(shape, axis):
    return lax.broadcasted_iota(I32, shape, axis)


def over(a, size, count):
    return sum(((a >= size * n).astype(I32) for n in range(1, count)), jnp.zeros(a.shape, I32))


def make_tables(tags, mine, per):
    ndev = tags.shape[0]
    each = per // 2
    bits = NY.bit_length() - 1
    tags, mine = (jnp.clip(a.astype(I32), 0, per - 1) for a in (tags, mine))
    sub, lane = iota((ndev, TWO), 0), iota((ndev, TWO), 1)
    piece_s, piece_l = over(sub, each, NY), over(lane, each, NY + 1)
    ids = [jnp.broadcast_to(tags[:, n : n + 1], (ndev, TWO)) for n in range(4)]
    rank_s = [(sub - each * piece_s) * 4 + n for n in range(4)]

    def top(terms, none):
        best = None
        for mask, rank in terms:
            new = jnp.where(mask, rank, -1)
            best = new if best is None else jnp.maximum(best, new)
        best = jnp.max(best, axis=0, keepdims=True)
        return jnp.where(best < 0, none, best)

    lane1, sub1 = iota((NY, TWO), 1), iota((NY, TWO), 0)
    block = jnp.zeros((NY, TWO), I32)
    for n in range(4):
        hit = ((lane1 >> bits) == n) & ((lane1 & (NY - 1)) == sub1)
        block = block + jnp.where(hit, jnp.broadcast_to(mine[:, n : n + 1], (NY, TWO)), 0)
    block = jnp.sum(block, axis=0, keepdims=True)
    lane0 = iota((1, TWO), 1)
    half = block & 1
    device = (lane0 & (NY - 1)) * each + (block >> 1)
    onto = []
    for s in range(2):
        chosen = jnp.where(half == 0, ids[s], ids[2 + s])
        onto.append(jnp.sum(jnp.where(sub == device, chosen, 0), axis=0, keepdims=True))
    count = 4 * NY
    sub2, lane2 = iota((count, TWO), 0), iota((count, TWO), 1)
    onto_s = [
        jnp.broadcast_to(jnp.sum(jnp.where(sub2 == lane2, onto[s], 0), axis=1, keepdims=True), (count, TWO))
        for s in range(2)
    ]

    def rank1(a, s):
        return ((a & (NY - 1)) * 4 + (a >> bits)) * 2 + s

    rows = [device, half]
    for s in range(2):
        rows.append(
            top(
                (((onto_s[t] == onto[s]) & (rank1(sub2, t) < rank1(lane2, s)), rank1(sub2, t)) for t in range(2)), 8 * NY
            )
        )
    rows.append(top(((onto_s[t] == lane2, rank1(sub2, t)) for t in range(2)), 8 * NY))
    for n in range(4):
        own = jnp.sum(jnp.where(sub == lane, ids[n], 0), axis=0, keepdims=True)
        rank_l = (lane - each * piece_l) * 4 + n
        rows.append(
            top(
                (((piece_s == piece_l) & (ids[m] == own) & (rank_s[m] < rank_l), rank_s[m]) for m in range(4)), 2 * per
            )
        )
    for g in range(-(-NY * per // TWO)):
        where = lane + g * TWO
        q = over(where, per, NY + 1)
        column = where - per * q
        rows.append(top((((piece_s == q) & (ids[m] == column), rank_s[m]) for m in range(4)), 2 * per))
    return rows + [jnp.zeros((1, TWO), I32)] * (TABLE - len(rows))


DEVICE, HALF, PREV1, LAST1, PREV2, LAST2, TABLE = 0, 1, 2, 4, 5, 9, 16


def purify(
    per, ids, counts, tile, keep_pattern, square, purified,
    panel, parts, row, early, late, first, second, total, keep, tags, table_v, table,
    z_sems, r_sems, x_sems, s_sems, y_sems, own_sem, table_sem,
):
    x, z, core, y = place()
    west, east = (z + NZ - 1) % NZ, (z + 1) % NZ
    south, north = (y + NY - 1) % NY, (y + 1) % NY
    before, after = (x + NX - 1) % NX, (x + 1) % NX
    twin = to(x, z, 1 - core, y)
    near = NY // 2
    z_hops = (NZ // 2, NZ - 1 - NZ // 2)
    r_hops = (near, NY - 1 - near)

    def y_hops(h):
        return r_hops if h % 2 == 0 else r_hops[::-1]

    started = []

    def start(c):
        c.start()
        started.append(c)

    def z_copy(g, way, hop):
        ref = (early, late)[g]
        slot = (z + NZ - hop) % NZ if way == 0 else (z + hop) % NZ
        return send(ref.at[slot], ref.at[slot], z_sems, (g, way, hop), to(x, east if way == 0 else west, core, y))

    def z_step(g, hop):
        for way in range(2):
            if 1 <= hop <= z_hops[way]:
                z_copy(g, way, hop - 1).wait_recv()
            if hop < z_hops[way]:
                start(z_copy(g, way, hop))

    def ring_y(ref, sems, at, way, hop):
        slot = (y + NY - hop) % NY if way == 0 else (y + hop) % NY
        return send(ref.at[slot], ref.at[slot], sems, at + (way, hop), to(x, z, core, north if way == 0 else south))

    def r_step(hop):
        for way in range(2):
            if 1 <= hop <= r_hops[way]:
                ring_y(row, r_sems, (), way, hop - 1).wait_recv()
            if hop < r_hops[way]:
                start(ring_y(row, r_sems, (), way, hop))

    def y_step(h, hop):
        for way in range(2):
            if 1 <= hop <= y_hops(h)[way]:
                ring_y(parts[h], y_sems, (h,), way, hop - 1).wait_recv()
            if hop < y_hops(h)[way]:
                start(ring_y(parts[h], y_sems, (h,), way, hop))

    def slab(h, at):
        return panel[h].at[pl.ds(at * NZ, NZ), core]

    def source(h):
        ref, at = (early, 2 * CP * h + (EXTRA if h else 0)) if h < AHEAD else (late, 2 * CP * (h - AHEAD))
        return ref.at[:, at : at + part_rows(h)]

    def x_copy(h, n):
        if n == 0:
            return send(source(h), slab(h, x), x_sems, (h, 0), to(after, z, core, y))
        if n == 1:
            return send(source(h), slab(h, x), x_sems, (h, 1), to(before, z, core, y))
        held = slab(h, jnp.where(core == 0, before, after))
        return send(held, held, x_sems, (h, 2), to(jnp.where(core == 0, after, before), z, core, y))

    def own_copy(h):
        return pltpu.make_async_copy(source(h), slab(h, x), own_sem.at[h])

    def s_copy(h, n):
        if n == 0:
            return send(source(h), slab(h, x), s_sems, (h, 0), twin)
        held = slab(h, (before, after, (x + 2) % NX)[n - 1])
        return send(held, held, s_sems, (h, n), twin)

    def x_begin(h):
        for n in range(2):
            start(x_copy(h, n))
        own_copy(h).start()
        start(s_copy(h, 0))

    def x_middle(h):
        for n in range(2):
            x_copy(h, n).wait_recv()
        start(x_copy(h, 2))
        for n in range(1, 3):
            start(s_copy(h, n))

    def x_end(h):
        x_copy(h, 2).wait_recv()
        start(s_copy(h, 3))
        own_copy(h).wait()
        for n in range(4):
            s_copy(h, n).wait_recv()

    greet(
        [to(after, z, core, y), to(before, z, core, y), to(x, west, core, y), to(x, east, core, y)]
        + [twin, to(x, z, core, south), to(x, z, core, north)]
    )

    at_row, at_lane = iota((TWO, TWO), 0), iota((TWO, TWO), 1)
    live = jnp.where(at_row < BLK, counts[0:1, 0:1], counts[1:2, 0:1])
    held = jnp.where((at_lane >= BLK).astype(I32) < live, tile[...], 0.0).T
    lane = iota((EXTRA, TWO), 1)
    mark = jnp.where(
        lane == 0,
        ids[0:1, 0:1],
        jnp.where(lane == 1, ids[0:1, 1:2], jnp.where(lane == 2, ids[1:2, 0:1], ids[1:2, 1:2])),
    ).astype(F32)
    row[y, :TWO] = held
    row[y, TWO:] = mark
    for h in range(NP):
        ref, at = (early, 2 * CP * h + (EXTRA if h else 0)) if h < AHEAD else (late, 2 * CP * (h - AHEAD))
        for s in range(2):
            ref[z, at + s * CP : at + (s + 1) * CP] = held[s * BLK + h * CP : s * BLK + (h + 1) * CP]
    early[z, 2 * CP : 2 * CP + EXTRA] = mark
    z_step(0, 0)
    r_step(0)

    first[8 * NY] = jnp.zeros((CP, TWO), F32)
    second[2 * per] = jnp.zeros((BLK, TWO), F32)
    square_iota = iota((per, per), 0) == iota((per, per), 1)
    keeps = [
        jnp.sum(jnp.where(square_iota, keep_pattern[r : r + 1, :], 0).astype(F32), axis=1, keepdims=True) for r in range(2)
    ]
    keep[...] = jnp.where(iota((per, TWO), 1) < BLK, keeps[0], keeps[1])

    for hop in range(1, max(NZ // 2, near) + 1):
        z_step(0, hop)
        r_step(hop)
    for h in range(AHEAD):
        x_begin(h)
    for hop in range(4):
        z_step(1, hop)
    x_middle(0)
    z_step(1, 4)
    z_step(1, 5)
    x_end(0)
    for hop in range(6, NZ // 2 + 1):
        z_step(1, hop)
    for h in range(AHEAD, NP):
        x_begin(h)

    def tag_row(n, _):
        for c in range(2):
            tags[pl.ds(2 * n + c, 1), :] = panel[0][n, c, 2 * CP : 2 * CP + 1, :]
        return 0

    lax.fori_loop(0, NX * NZ, tag_row, 0)
    mine = jnp.concatenate([row[q, TWO : TWO + 1, :] for q in range(NY)], axis=0)
    for n, line in enumerate(make_tables(tags[...], mine, per)):
        table_v[n : n + 1, :] = line
    fetch = pltpu.make_async_copy(table_v, table, table_sem)
    fetch.start()
    fetch.wait()

    bits = NY.bit_length() - 1
    lanes = iota((2 * CP, TWO), 1) // BLK
    side = iota((CP, TWO), 1) // BLK

    def first_part(h):
        def one_panel(q, _):
            high_w, low_w = split(row[q, :TWO])
            wide = jnp.concatenate([high_w, low_w], axis=1)
            stack = []
            for n in range(4):
                e = (n << bits) + q
                device = table[DEVICE, e]
                block = panel[h][device // 2, device % 2, : 2 * CP, :]
                block = jnp.where(table[HALF, e] == n % 2, block, pltpu.roll(block, BLK, 1))
                stack.append(jnp.where(lanes == n % 2, block, 0.0))
            high, low = split(jnp.concatenate(stack, axis=0))
            both = dot(high, wide)
            made = both[:, :TWO] + both[:, TWO:] + dot(low, high_w)
            for n in range(8):
                term = jnp.where(side == n // 4, made[n * CP : (n + 1) * CP], 0.0)
                first[q * 8 + n] = term + first[table[PREV1 + n % 2, ((n // 2) << bits) + q]]
            return 0

        lax.fori_loop(0, NY, one_panel, 0)

        def one_column(j, _):
            parts[h][y, j] = first[table[LAST1, j]] * keep[pl.ds(j, 1), :]
            return 0

        lax.fori_loop(0, per, one_column, 0)

    quarter = BLK // 2

    def half_pass(q, half, fresh):
        here = range(half * NP // 2, (half + 1) * NP // 2)
        inside = (iota((TWO, TWO), 1) % BLK) // quarter == half

        def one_device(d, _):
            device = q * (per // 2) + d
            block = jnp.concatenate([panel[h][device // 2, device % 2, : 2 * CP, :] for h in range(NP)], axis=0)
            high = block.astype(BF16)
            rough = high.astype(F32)
            rest = pltpu.roll(block - rough, quarter if half == 0 else TWO - quarter, 1)
            mixed = jnp.where(inside, rough, rest).astype(BF16)
            none = jnp.zeros((BLK, TWO), BF16)
            blank = jnp.zeros((quarter, TWO), BF16)
            upper, lower = [], []
            for r in range(2):
                high_w, low_w = split(jnp.concatenate([parts[h][q, d * 2 + r] for h in here], axis=0))
                twice = jnp.concatenate([high_w, high_w], axis=0)
                once = jnp.concatenate([low_w, blank] if half == 0 else [blank, low_w], axis=0)
                upper.append(jnp.concatenate([twice, none] if r == 0 else [none, twice], axis=1))
                lower.append(jnp.concatenate([once, none] if r == 0 else [none, once], axis=1))
            made = dot(jnp.concatenate([mixed, high], axis=1), jnp.concatenate(upper + lower, axis=0))
            for r in range(2):
                for s in range(2):
                    term = jnp.concatenate(
                        [made[(h * 2 + s) * CP : (h * 2 + s + 1) * CP, r * TWO : (r + 1) * TWO] for h in range(NP)],
                        axis=0,
                    )
                    second[d * 4 + r * 2 + s] = term + second[table[PREV2 + r * 2 + s, device]]
            return 0

        lax.fori_loop(0, per // 2, one_device, 0)

        def one_column(j, _):
            at = q * per + j
            new = second[table[LAST2 + at // TWO, at % TWO]]
            total[j] = new if fresh else total[j] + new
            return 0

        lax.fori_loop(0, per, one_column, 0)

    def own(pair):
        return jnp.concatenate([parts[h][y, pair * 2 + b] for b in range(2) for h in range(NP)], axis=0)

    def arrived(hop, half):
        half_pass((y + NY - hop) % NY, half, False)
        if 2 * hop < NY:
            half_pass((y + hop) % NY, half, False)

    for tick in range(NP + near):
        if 1 <= tick < NP:
            x_end(tick)
        if tick < NP:
            first_part(tick)
            y_step(tick, 0)
        if tick + 1 < NP:
            x_middle(tick + 1)
        for hop in range(1, near + 1):
            if 0 <= tick - hop < NP:
                y_step(tick - hop, hop)
        if tick == NP - 1:
            half_pass(y, 0, True)
            arrived(1, 0)
        if NP <= tick <= NP + near - 2:
            arrived(tick - NP + 2, 0)
        if tick == NP:
            half_pass(y, 1, False)
            for pair in range(per // 2):
                square[:, pair * TWO : (pair + 1) * TWO] = own(pair).T
        if tick >= NP:
            arrived(tick - NP + 1, 1)
    for pair in range(per // 2):
        cube = jnp.concatenate(
            [total[pair * 2 + b] * keep[pair * 2 + b : pair * 2 + b + 1, :] for b in range(2)], axis=0
        )
        purified[:, pair * TWO : (pair + 1) * TWO] = (3.0 * own(pair) - 2.0 * cube).T
    for c in started:
        c.wait_send()


def local(values, column_ids, counts, keep_pattern):
    per = keep_pattern.shape[1]
    ndev = NX * NZ * 2
    vmem = pl.BlockSpec(memory_space=pltpu.VMEM)

    def dma(*shape):
        return [pltpu.SemaphoreType.DMA(shape), pltpu.SemaphoreType.DMA(shape)]

    def body(ids, counts, tile, keep_pattern, square, purified, *rest):
        panel, parts, others, sems = rest[:NP], rest[NP : 2 * NP], rest[2 * NP : 2 * NP + 10], rest[2 * NP + 10 :]
        pairs = [sems[2 * n : 2 * n + 2] for n in range(5)]
        purify(
            per, ids, counts, tile, keep_pattern, square, purified, panel, parts, *others, *pairs, sems[10], sems[11]
        )

    out = jax.ShapeDtypeStruct((TWO, per * BLK), F32)
    return pl.pallas_call(
        body,
        out_shape=(out, out),
        in_specs=[vmem] * 4,
        out_specs=(vmem, vmem),
        scratch_shapes=[pltpu.VMEM((NX * NZ, 2, part_rows(h), TWO), F32) for h in range(NP)]
        + [pltpu.VMEM((NY, per, CP, TWO), F32) for _ in range(NP)]
        + [
            pltpu.VMEM((NY, TWO + EXTRA, TWO), F32),
            pltpu.VMEM((NZ, 2 * CP * AHEAD + EXTRA, TWO), F32),
            pltpu.VMEM((NZ, 2 * CP * (NP - AHEAD), TWO), F32),
            pltpu.VMEM((8 * NY + 1, CP, TWO), F32),
            pltpu.VMEM((2 * per + 1, BLK, TWO), F32),
            pltpu.VMEM((per, BLK, TWO), F32),
            pltpu.VMEM((per, TWO), F32),
            pltpu.VMEM((ndev, TWO), F32),
            pltpu.VMEM((TABLE, TWO), I32),
            pltpu.SMEM((TABLE, TWO), I32),
        ]
        + dma(2, 2, NZ) + dma(2, NY) + dma(NP, 3) + dma(NP, 4) + dma(NP, 2, NY)
        + [pltpu.SemaphoreType.DMA((NP,)), pltpu.SemaphoreType.DMA],
        compiler_params=pltpu.CompilerParams(collective_id=0, has_side_effects=True, vmem_limit_bytes=48 << 20),
        name="purify",
    )(column_ids, counts, values, keep_pattern)


def solution(mesh):
    return jax.shard_map(
        local,
        mesh=mesh,
        in_specs=(P("row", "col"), P("row", "col"), P("row", "col"), P("row", "col")),
        out_specs=(P("row", "col"), P("row", "col")),
        check_vma=False,
    )
```

```python
import jax
import jax.numpy as jnp
from jax import lax
from jax.experimental import pallas as pl
from jax.experimental.pallas import tpu as pltpu
from jax.sharding import PartitionSpec as P

MESH = pl.DeviceIdType.MESH
NX, NZ, NY = 4, 12, 8
BLK = 64
TWO = 2 * BLK
WIDTHS = (16, 16, 16, 16)
LONGER = (0, 1, 0, 1)
NP = len(WIDTHS)
AT = tuple(sum(WIDTHS[:h]) for h in range(NP))
AHEAD = 2
ROWS = tuple(2 * AT[h] - (2 * AT[AHEAD] if h >= AHEAD else 2 * AT[h]) for h in range(NP))
EXTRA = 8
F32, BF16, I32 = jnp.float32, jnp.bfloat16, jnp.int32


def place():
    row, col = lax.axis_index("row"), lax.axis_index("col")
    return row // (2 * NZ), (row // 2) % NZ, row % 2, col


def to(x, z, core, y):
    return ((x * NZ + z) * 2 + core, y)


def greet(partners):
    barrier = pltpu.get_barrier_semaphore()
    for partner in partners:
        pl.semaphore_signal(barrier, inc=1, device_id=partner, device_id_type=MESH)
    pl.semaphore_wait(barrier, len(partners))


def send(src, dst, sems, at, target):
    return pltpu.make_async_remote_copy(
        src_ref=src, dst_ref=dst, send_sem=sems[0].at[at], recv_sem=sems[1].at[at], device_id=target, device_id_type=MESH
    )


def split(a):
    high = a.astype(BF16)
    return high, (a - high.astype(F32)).astype(BF16)


def dot(a, b):
    return jnp.dot(a, b, preferred_element_type=F32)


def part_rows(h):
    return 2 * WIDTHS[h] + (EXTRA if h == 0 else 0)


def iota(shape, axis):
    return lax.broadcasted_iota(I32, shape, axis)


def over(a, size, count):
    return sum(((a >= size * n).astype(I32) for n in range(1, count)), jnp.zeros(a.shape, I32))


def make_tables(tags, mine, per):
    ndev = tags.shape[0]
    each = per // 2
    bits = NY.bit_length() - 1
    tags, mine = (jnp.clip(a.astype(I32), 0, per - 1) for a in (tags, mine))
    sub, lane = iota((ndev, TWO), 0), iota((ndev, TWO), 1)
    piece_s, piece_l = over(sub, each, NY), over(lane, each, NY + 1)
    ids = [jnp.broadcast_to(tags[:, n : n + 1], (ndev, TWO)) for n in range(4)]
    rank_s = [(sub - each * piece_s) * 4 + n for n in range(4)]

    def top(terms, none):
        best = None
        for mask, rank in terms:
            new = jnp.where(mask, rank, -1)
            best = new if best is None else jnp.maximum(best, new)
        best = jnp.max(best, axis=0, keepdims=True)
        return jnp.where(best < 0, none, best)

    lane1, sub1 = iota((NY, TWO), 1), iota((NY, TWO), 0)
    block = jnp.zeros((NY, TWO), I32)
    for n in range(4):
        hit = ((lane1 >> bits) == n) & ((lane1 & (NY - 1)) == sub1)
        block = block + jnp.where(hit, jnp.broadcast_to(mine[:, n : n + 1], (NY, TWO)), 0)
    block = jnp.sum(block, axis=0, keepdims=True)
    lane0 = iota((1, TWO), 1)
    half = block & 1
    device = (lane0 & (NY - 1)) * each + (block >> 1)
    onto = []
    for s in range(2):
        chosen = jnp.where(half == 0, ids[s], ids[2 + s])
        onto.append(jnp.sum(jnp.where(sub == device, chosen, 0), axis=0, keepdims=True))
    count = 4 * NY
    sub2, lane2 = iota((count, TWO), 0), iota((count, TWO), 1)
    onto_s = [
        jnp.broadcast_to(jnp.sum(jnp.where(sub2 == lane2, onto[s], 0), axis=1, keepdims=True), (count, TWO))
        for s in range(2)
    ]

    def rank1(a, s):
        return ((a & (NY - 1)) * 4 + (a >> bits)) * 2 + s

    along_x = over(device, 2 * NZ, NX)
    along_z = (device - 2 * NZ * along_x) >> 1
    rows = [along_x, half]
    for s in range(2):
        rows.append(
            top(
                (((onto_s[t] == onto[s]) & (rank1(sub2, t) < rank1(lane2, s)), rank1(sub2, t)) for t in range(2)), 8 * NY
            )
        )
    rows.append(top(((onto_s[t] == lane2, rank1(sub2, t)) for t in range(2)), 8 * NY))
    for n in range(4):
        own = jnp.sum(jnp.where(sub == lane, ids[n], 0), axis=0, keepdims=True)
        rank_l = (lane - each * piece_l) * 4 + n
        rows.append(
            top(
                (((piece_s == piece_l) & (ids[m] == own) & (rank_s[m] < rank_l), rank_s[m]) for m in range(4)), 2 * per
            )
        )
    for g in range(-(-NY * per // TWO)):
        where = lane + g * TWO
        q = over(where, per, NY + 1)
        column = where - per * q
        rows.append(top((((piece_s == q) & (ids[m] == column), rank_s[m]) for m in range(4)), 2 * per))
    blank = jnp.zeros((1, TWO), I32)
    rows = rows + [blank] * (ZS - len(rows)) + [along_z, device & 1]
    return rows + [blank] * (TABLE - len(rows))


XS, HALF, PREV1, LAST1, PREV2, LAST2, ZS, CORES, TABLE = 0, 1, 2, 4, 5, 9, 11, 12, 16


def purify(
    per, ids, counts, tile, keep_pattern, square, purified,
    panel, parts, row, early, first, second, total, keep, tags, table_v, table,
    z_sems, r_sems, x_sems, s_sems, y_sems, w_sems, t_sems, own_sem, table_sem,
):
    x, z, core, y = place()
    west, east = (z + NZ - 1) % NZ, (z + 1) % NZ
    south, north = (y + NY - 1) % NY, (y + 1) % NY
    before, after = (x + NX - 1) % NX, (x + 1) % NX
    twin = to(x, z, 1 - core, y)
    near = NY // 2
    wide = panel[AHEAD]
    z_hops = (NZ // 2, NZ - 1 - NZ // 2)
    r_hops = (near, NY - 1 - near)

    def y_hops(h):
        return r_hops if LONGER[h] == 0 else r_hops[::-1]

    started = []

    def start(c):
        c.start()
        started.append(c)

    def z_copy(g, way, hop):
        slot = (z + NZ - hop) % NZ if way == 0 else (z + hop) % NZ
        ref = early.at[slot] if g == 0 else wide.at[:, slot, core]
        return send(ref, ref, z_sems, (g, way, hop), to(x, east if way == 0 else west, core, y))

    def z_step(g, hop):
        for way in range(2):
            if 1 <= hop <= z_hops[way]:
                z_copy(g, way, hop - 1).wait_recv()
            if hop < z_hops[way]:
                start(z_copy(g, way, hop))

    def ring_y(ref, sems, at, way, hop):
        slot = (y + NY - hop) % NY if way == 0 else (y + hop) % NY
        return send(ref.at[slot], ref.at[slot], sems, at + (way, hop), to(x, z, core, north if way == 0 else south))

    def r_step(hop):
        for way in range(2):
            if 1 <= hop <= r_hops[way]:
                ring_y(row, r_sems, (), way, hop - 1).wait_recv()
            if hop < r_hops[way]:
                start(ring_y(row, r_sems, (), way, hop))

    def y_step(h, hop):
        for way in range(2):
            if 1 <= hop <= y_hops(h)[way]:
                ring_y(parts[h], y_sems, (h,), way, hop - 1).wait_recv()
            if hop < y_hops(h)[way]:
                start(ring_y(parts[h], y_sems, (h,), way, hop))

    def slab(h, at):
        return panel[h].at[at, :, core]

    def source(h):
        at = sum(part_rows(g) for g in range(h))
        return early.at[:, at : at + part_rows(h)]

    def x_copy(h, n):
        if n == 0:
            return send(source(h), slab(h, x), x_sems, (h, 0), to(after, z, core, y))
        if n == 1:
            return send(source(h), slab(h, x), x_sems, (h, 1), to(before, z, core, y))
        held = slab(h, jnp.where(core == 0, before, after))
        return send(held, held, x_sems, (h, 2), to(jnp.where(core == 0, after, before), z, core, y))

    def own_copy(h):
        return pltpu.make_async_copy(source(h), slab(h, x), own_sem.at[h])

    def s_copy(h, n):
        if n == 0:
            return send(source(h), slab(h, x), s_sems, (h, 0), twin)
        held = slab(h, (before, after, (x + 2) % NX)[n - 1])
        return send(held, held, s_sems, (h, n), twin)

    def x_begin(h):
        for n in range(2):
            start(x_copy(h, n))
        own_copy(h).start()
        start(s_copy(h, 0))

    def x_middle(h):
        for n in range(2):
            x_copy(h, n).wait_recv()
        start(x_copy(h, 2))
        for n in range(1, 3):
            start(s_copy(h, n))

    def x_end(h):
        x_copy(h, 2).wait_recv()
        start(s_copy(h, 3))
        own_copy(h).wait()
        for n in range(4):
            s_copy(h, n).wait_recv()

    def w_copy(n):
        at = (x, x, jnp.where(core == 0, before, after))[n]
        target = (after, before, jnp.where(core == 0, after, before))[n]
        return send(wide.at[at, z, core], wide.at[at, z, core], w_sems, (n,), to(target, z, core, y))

    def t_copy(n, slot):
        return send(wide.at[:, slot, core], wide.at[:, slot, core], t_sems, (n,), twin)

    def w_step(hop):
        z_step(1, hop)
        if hop == 0:
            start(t_copy(0, z))
        for way in range(2):
            if 1 <= hop <= z_hops[way]:
                start(t_copy(hop, (z + NZ - hop) % NZ) if way == 0 else t_copy(NZ - hop, (z + hop) % NZ))

    def w_end():
        for n in range(NZ):
            t_copy(n, z).wait_recv()

    greet(
        [to(after, z, core, y), to(before, z, core, y), to(x, west, core, y), to(x, east, core, y)]
        + [twin, to(x, z, core, south), to(x, z, core, north)]
    )

    at_row, at_lane = iota((TWO, TWO), 0), iota((TWO, TWO), 1)
    live = jnp.where(at_row < BLK, counts[0:1, 0:1], counts[1:2, 0:1])
    held = jnp.where((at_lane >= BLK).astype(I32) < live, tile[...], 0.0).T
    lane = iota((EXTRA, TWO), 1)
    mark = jnp.where(
        lane == 0,
        ids[0:1, 0:1],
        jnp.where(lane == 1, ids[0:1, 1:2], jnp.where(lane == 2, ids[1:2, 0:1], ids[1:2, 1:2])),
    ).astype(F32)
    row[y, :TWO] = held
    row[y, TWO:] = mark
    for h in range(NP):
        for s in range(2):
            chunk = held[s * BLK + AT[h] : s * BLK + AT[h] + WIDTHS[h]]
            if h < AHEAD:
                at = sum(part_rows(g) for g in range(h)) + s * WIDTHS[h]
                early[z, at : at + WIDTHS[h]] = chunk
            else:
                at = ROWS[h] + s * WIDTHS[h]
                wide[x, z, core, at : at + WIDTHS[h]] = chunk
    early[z, 2 * WIDTHS[0] : 2 * WIDTHS[0] + EXTRA] = mark
    z_step(0, 0)
    r_step(0)
    for n in range(2):
        start(w_copy(n))

    first[8 * NY] = jnp.zeros((max(WIDTHS), TWO), F32)
    second[2 * per] = jnp.zeros((BLK, TWO), F32)
    square_iota = iota((per, per), 0) == iota((per, per), 1)
    keeps = [
        jnp.sum(jnp.where(square_iota, keep_pattern[r : r + 1, :], 0).astype(F32), axis=1, keepdims=True) for r in range(2)
    ]
    keep[...] = jnp.where(iota((per, TWO), 1) < BLK, keeps[0], keeps[1])

    for hop in range(1, max(NZ // 2, near) + 1):
        z_step(0, hop)
        r_step(hop)
        if hop == 1:
            for n in range(2):
                w_copy(n).wait_recv()
            start(w_copy(2))
        if hop == 2:
            w_copy(2).wait_recv()
            w_step(0)
        if hop in (4, 5):
            w_step(hop - 3)
    x_begin(0)
    w_step(3)
    x_middle(0)
    x_begin(1)
    w_step(4)
    x_end(0)

    def tag_row(n, _):
        for c in range(2):
            tags[pl.ds(2 * n + c, 1), :] = panel[0][n // NZ, n % NZ, c, 2 * WIDTHS[0] : 2 * WIDTHS[0] + 1, :]
        return 0

    lax.fori_loop(0, NX * NZ, tag_row, 0)
    mine = jnp.concatenate([row[q, TWO : TWO + 1, :] for q in range(NY)], axis=0)
    for n, line in enumerate(make_tables(tags[...], mine, per)):
        table_v[n : n + 1, :] = line
    fetch = pltpu.make_async_copy(table_v, table, table_sem)
    fetch.start()
    fetch.wait()

    bits = NY.bit_length() - 1

    def block_of(h, along_x, along_z, side):
        return panel[min(h, AHEAD)][along_x, along_z, side, ROWS[h] : ROWS[h] + 2 * WIDTHS[h], :]

    def first_part(h):
        cp = WIDTHS[h]
        lanes = iota((2 * cp, TWO), 1) // BLK
        side = iota((cp, TWO), 1) // BLK

        def one_panel(q, _):
            high_w, low_w = split(row[q, :TWO])
            wide = jnp.concatenate([high_w, low_w], axis=1)
            stack = []
            for n in range(4):
                e = (n << bits) + q
                block = block_of(h, table[XS, e], table[ZS, e], table[CORES, e])
                block = jnp.where(table[HALF, e] == n % 2, block, pltpu.roll(block, BLK, 1))
                stack.append(jnp.where(lanes == n % 2, block, 0.0))
            high, low = split(jnp.concatenate(stack, axis=0))
            both = dot(high, wide)
            made = both[:, :TWO] + both[:, TWO:] + dot(low, high_w)
            for n in range(8):
                term = jnp.where(side == n // 4, made[n * cp : (n + 1) * cp], 0.0)
                first[q * 8 + n, :cp, :] = term + first[table[PREV1 + n % 2, ((n // 2) << bits) + q], :cp, :]
            return 0

        lax.fori_loop(0, NY, one_panel, 0)

        def one_column(j, _):
            parts[h][y, j] = first[table[LAST1, j], :cp, :] * keep[pl.ds(j, 1), :]
            return 0

        lax.fori_loop(0, per, one_column, 0)

    def second_pass(q, fresh):
        def one_device(d, _):
            device = q * (per // 2) + d
            spot = (device // (2 * NZ), (device // 2) % NZ, device % 2)
            high, low = split(jnp.concatenate([block_of(h, *spot) for h in range(NP)], axis=0))
            none = jnp.zeros((BLK, TWO), BF16)
            upper, lower = [], []
            for r in range(2):
                pieces = split(jnp.concatenate([parts[h][q, d * 2 + r] for h in range(NP)], axis=0))
                for side, piece in zip((upper, lower), pieces):
                    side.append(jnp.concatenate([piece, none] if r == 0 else [none, piece], axis=1))
            made = dot(jnp.concatenate([high, low], axis=1), jnp.concatenate(upper + upper, axis=0))
            made = made + dot(high, jnp.concatenate(lower, axis=0))
            for r in range(2):
                for s in range(2):
                    term = jnp.concatenate(
                        [
                            made[2 * AT[h] + s * WIDTHS[h] : 2 * AT[h] + (s + 1) * WIDTHS[h], r * TWO : (r + 1) * TWO]
                            for h in range(NP)
                        ],
                        axis=0,
                    )
                    second[d * 4 + r * 2 + s] = term + second[table[PREV2 + r * 2 + s, device]]
            return 0

        lax.fori_loop(0, per // 2, one_device, 0)

        def one_column(j, _):
            at = q * per + j
            new = second[table[LAST2 + at // TWO, at % TWO]]
            total[j] = new if fresh else total[j] + new
            return 0

        lax.fori_loop(0, per, one_column, 0)

    def own(pair):
        return jnp.concatenate([parts[h][y, pair * 2 + b] for b in range(2) for h in range(NP)], axis=0)

    def arrive(*steps):
        for h, hop in steps:
            y_step(h, hop)

    def form(h):
        first_part(h)
        y_step(h, 0)

    form(0)
    w_step(5)
    x_middle(1)
    for hop in range(6, NZ // 2 + 1):
        w_step(hop)
    x_end(1)
    form(1)
    w_end()
    form(2)
    arrive((0, 1))
    form(3)
    arrive((1, 1))
    second_pass(y, True)
    for hop in range(1, near + 1):
        if hop > 1:
            arrive((0, hop), (1, hop))
            second_pass((y + hop - 1) % NY, False)
        if hop == near:
            for pair in range(per // 2):
                square[:, pair * TWO : (pair + 1) * TWO] = own(pair).T
        arrive((2, hop), (3, hop))
        second_pass((y + NY - hop) % NY, False)
    for pair in range(per // 2):
        cube = jnp.concatenate(
            [total[pair * 2 + b] * keep[pair * 2 + b : pair * 2 + b + 1, :] for b in range(2)], axis=0
        )
        purified[:, pair * TWO : (pair + 1) * TWO] = (3.0 * own(pair) - 2.0 * cube).T
    for c in started:
        c.wait_send()


def local(values, column_ids, counts, keep_pattern):
    per = keep_pattern.shape[1]
    ndev = NX * NZ * 2
    vmem = pl.BlockSpec(memory_space=pltpu.VMEM)

    def dma(*shape):
        return [pltpu.SemaphoreType.DMA(shape), pltpu.SemaphoreType.DMA(shape)]

    held = AHEAD + 1

    def body(ids, counts, tile, keep_pattern, square, purified, *rest):
        panel, parts, others, sems = rest[:held], rest[held : held + NP], rest[held + NP : held + NP + 9], rest[held + NP + 9 :]
        pairs = [sems[2 * n : 2 * n + 2] for n in range(7)]
        purify(
            per, ids, counts, tile, keep_pattern, square, purified, panel, parts, *others, *pairs, sems[14], sems[15]
        )

    out = jax.ShapeDtypeStruct((TWO, per * BLK), F32)
    return pl.pallas_call(
        body,
        out_shape=(out, out),
        in_specs=[vmem] * 4,
        out_specs=(vmem, vmem),
        scratch_shapes=[pltpu.VMEM((NX, NZ, 2, part_rows(h), TWO), F32) for h in range(AHEAD)]
        + [pltpu.VMEM((NX, NZ, 2, sum(part_rows(h) for h in range(AHEAD, NP)), TWO), F32)]
        + [pltpu.VMEM((NY, per, WIDTHS[h], TWO), F32) for h in range(NP)]
        + [
            pltpu.VMEM((NY, TWO + EXTRA, TWO), F32),
            pltpu.VMEM((NZ, sum(part_rows(h) for h in range(AHEAD)), TWO), F32),
            pltpu.VMEM((8 * NY + 1, max(WIDTHS), TWO), F32),
            pltpu.VMEM((2 * per + 1, BLK, TWO), F32),
            pltpu.VMEM((per, BLK, TWO), F32),
            pltpu.VMEM((per, TWO), F32),
            pltpu.VMEM((ndev, TWO), F32),
            pltpu.VMEM((TABLE, TWO), I32),
            pltpu.SMEM((TABLE, TWO), I32),
        ]
        + dma(2, 2, NZ) + dma(2, NY) + dma(AHEAD, 3) + dma(AHEAD, 4) + dma(NP, 2, NY) + dma(3) + dma(NZ)
        + [pltpu.SemaphoreType.DMA((AHEAD,)), pltpu.SemaphoreType.DMA],
        compiler_params=pltpu.CompilerParams(collective_id=0, has_side_effects=True, vmem_limit_bytes=48 << 20),
        name="purify",
    )(column_ids, counts, values, keep_pattern)


def solution(mesh):
    return jax.shard_map(
        local,
        mesh=mesh,
        in_specs=(P("row", "col"), P("row", "col"), P("row", "col"), P("row", "col")),
        out_specs=(P("row", "col"), P("row", "col")),
        check_vma=False,
    )
```

```python
import jax
import jax.numpy as jnp
from jax import lax
from jax.experimental import pallas as pl
from jax.experimental.pallas import tpu as pltpu
from jax.sharding import PartitionSpec as P

MESH = pl.DeviceIdType.MESH
NX, NZ, NY = 4, 12, 8
BLK = 64
TWO = 2 * BLK
WIDTHS = (16, 16, 16, 16)
LONGER = (0, 1, 0, 1)
NP = len(WIDTHS)
AT = tuple(sum(WIDTHS[:h]) for h in range(NP))
AHEAD = 2
ROWS = tuple(2 * AT[h] - (2 * AT[AHEAD] if h >= AHEAD else 2 * AT[h]) for h in range(NP))
EXTRA = 8
F32, BF16, I32 = jnp.float32, jnp.bfloat16, jnp.int32


def place():
    row, col = lax.axis_index("row"), lax.axis_index("col")
    return row // (2 * NZ), (row // 2) % NZ, row % 2, col


def to(x, z, core, y):
    return ((x * NZ + z) * 2 + core, y)


def greet(partners):
    barrier = pltpu.get_barrier_semaphore()
    for partner in partners:
        pl.semaphore_signal(barrier, inc=1, device_id=partner, device_id_type=MESH)
    pl.semaphore_wait(barrier, len(partners))


def send(src, dst, sems, at, target):
    return pltpu.make_async_remote_copy(
        src_ref=src, dst_ref=dst, send_sem=sems[0].at[at], recv_sem=sems[1].at[at], device_id=target, device_id_type=MESH
    )


def split(a):
    high = a.astype(BF16)
    return high, (a - high.astype(F32)).astype(BF16)


def dot(a, b):
    return jnp.dot(a, b, preferred_element_type=F32)


def part_rows(h):
    return 2 * WIDTHS[h] + (EXTRA if h == 0 else 0)


def iota(shape, axis):
    return lax.broadcasted_iota(I32, shape, axis)


def over(a, size, count):
    return sum(((a >= size * n).astype(I32) for n in range(1, count)), jnp.zeros(a.shape, I32))


def make_tables(tags, mine, per):
    ndev = tags.shape[0]
    each = per // 2
    bits = NY.bit_length() - 1
    tags, mine = (jnp.clip(a.astype(I32), 0, per - 1) for a in (tags, mine))
    sub, lane = iota((ndev, TWO), 0), iota((ndev, TWO), 1)
    piece_s, piece_l = over(sub, each, NY), over(lane, each, NY + 1)
    ids = [jnp.broadcast_to(tags[:, n : n + 1], (ndev, TWO)) for n in range(4)]
    rank_s = [(sub - each * piece_s) * 4 + n for n in range(4)]

    def top(terms, none):
        best = None
        for mask, rank in terms:
            new = jnp.where(mask, rank, -1)
            best = new if best is None else jnp.maximum(best, new)
        best = jnp.max(best, axis=0, keepdims=True)
        return jnp.where(best < 0, none, best)

    lane1, sub1 = iota((NY, TWO), 1), iota((NY, TWO), 0)
    block = jnp.zeros((NY, TWO), I32)
    for n in range(4):
        hit = ((lane1 >> bits) == n) & ((lane1 & (NY - 1)) == sub1)
        block = block + jnp.where(hit, jnp.broadcast_to(mine[:, n : n + 1], (NY, TWO)), 0)
    block = jnp.sum(block, axis=0, keepdims=True)
    lane0 = iota((1, TWO), 1)
    half = block & 1
    device = (lane0 & (NY - 1)) * each + (block >> 1)
    onto = []
    for s in range(2):
        chosen = jnp.where(half == 0, ids[s], ids[2 + s])
        onto.append(jnp.sum(jnp.where(sub == device, chosen, 0), axis=0, keepdims=True))
    count = 4 * NY
    sub2, lane2 = iota((count, TWO), 0), iota((count, TWO), 1)
    onto_s = [
        jnp.broadcast_to(jnp.sum(jnp.where(sub2 == lane2, onto[s], 0), axis=1, keepdims=True), (count, TWO))
        for s in range(2)
    ]

    def rank1(a, s):
        return ((a & (NY - 1)) * 4 + (a >> bits)) * 2 + s

    along_x = over(device, 2 * NZ, NX)
    along_z = (device - 2 * NZ * along_x) >> 1
    rows = [along_x, half]
    for s in range(2):
        rows.append(
            top(
                (((onto_s[t] == onto[s]) & (rank1(sub2, t) < rank1(lane2, s)), rank1(sub2, t)) for t in range(2)), 8 * NY
            )
        )
    rows.append(top(((onto_s[t] == lane2, rank1(sub2, t)) for t in range(2)), 8 * NY))
    for n in range(4):
        own = jnp.sum(jnp.where(sub == lane, ids[n], 0), axis=0, keepdims=True)
        rank_l = (lane - each * piece_l) * 4 + n
        rows.append(
            top(
                (((piece_s == piece_l) & (ids[m] == own) & (rank_s[m] < rank_l), rank_s[m]) for m in range(4)), 2 * per
            )
        )
    for g in range(-(-NY * per // TWO)):
        where = lane + g * TWO
        q = over(where, per, NY + 1)
        column = where - per * q
        rows.append(top((((piece_s == q) & (ids[m] == column), rank_s[m]) for m in range(4)), 2 * per))
    blank = jnp.zeros((1, TWO), I32)
    rows = rows + [blank] * (ZS - len(rows)) + [along_z, device & 1]
    return rows + [blank] * (TABLE - len(rows))


XS, HALF, PREV1, LAST1, PREV2, LAST2, ZS, CORES, TABLE = 0, 1, 2, 4, 5, 9, 11, 12, 16


def purify(
    per, ids, counts, tile, keep_pattern, square, purified,
    panel, parts, row, early, first, second, total, keep, tags, table_v, table,
    z_sems, r_sems, x_sems, s_sems, y_sems, w_sems, t_sems, c_sems, own_sem, table_sem,
):
    x, z, core, y = place()
    west, east = (z + NZ - 1) % NZ, (z + 1) % NZ
    south, north = (y + NY - 1) % NY, (y + 1) % NY
    before, after = (x + NX - 1) % NX, (x + 1) % NX
    twin = to(x, z, 1 - core, y)
    near = NY // 2
    wide = panel[AHEAD]
    z_hops = (NZ // 2, NZ - 1 - NZ // 2)
    r_hops = (near, NY - 1 - near)

    def y_hops(h):
        return r_hops if LONGER[h] == 0 else r_hops[::-1]

    started = []

    def start(c):
        c.start()
        started.append(c)

    def z_copy(g, way, hop):
        slot = (z + NZ - hop) % NZ if way == 0 else (z + hop) % NZ
        ref = (panel[0].at[x, slot, core], wide.at[:, slot, core], early.at[slot])[g]
        return send(ref, ref, z_sems, (g, way, hop), to(x, east if way == 0 else west, core, y))

    def z_step(g, hop):
        for way in range(2):
            if 1 <= hop <= z_hops[way]:
                z_copy(g, way, hop - 1).wait_recv()
            if hop < z_hops[way]:
                start(z_copy(g, way, hop))

    def ring_y(ref, sems, at, way, hop):
        slot = (y + NY - hop) % NY if way == 0 else (y + hop) % NY
        return send(ref.at[slot], ref.at[slot], sems, at + (way, hop), to(x, z, core, north if way == 0 else south))

    def r_step(hop):
        for way in range(2):
            if 1 <= hop <= r_hops[way]:
                ring_y(row, r_sems, (), way, hop - 1).wait_recv()
            if hop < r_hops[way]:
                start(ring_y(row, r_sems, (), way, hop))

    def y_step(h, hop):
        for way in range(2):
            if 1 <= hop <= y_hops(h)[way]:
                ring_y(parts[h], y_sems, (h,), way, hop - 1).wait_recv()
            if hop < y_hops(h)[way]:
                start(ring_y(parts[h], y_sems, (h,), way, hop))

    def slab(h, at):
        return panel[h].at[at, :, core]

    def source(h):
        at = sum(part_rows(g) for g in range(1, h))
        return early.at[:, at : at + part_rows(h)]

    def x_copy(h, n):
        if n == 0:
            return send(source(h), slab(h, x), x_sems, (h, 0), to(after, z, core, y))
        if n == 1:
            return send(source(h), slab(h, x), x_sems, (h, 1), to(before, z, core, y))
        held = slab(h, jnp.where(core == 0, before, after))
        return send(held, held, x_sems, (h, 2), to(jnp.where(core == 0, after, before), z, core, y))

    def own_copy(h):
        return pltpu.make_async_copy(source(h), slab(h, x), own_sem.at[h])

    def s_copy(h, n):
        if n == 0 and h > 0:
            return send(source(h), slab(h, x), s_sems, (h, 0), twin)
        held = slab(h, (x, before, after, (x + 2) % NX)[n])
        return send(held, held, s_sems, (h, n), twin)

    def x_begin(h):
        for n in range(2):
            start(x_copy(h, n))
        own_copy(h).start()
        start(s_copy(h, 0))

    def x_middle(h):
        for n in range(2):
            x_copy(h, n).wait_recv()
        start(x_copy(h, 2))
        for n in range(1, 3):
            start(s_copy(h, n))

    def x_end(h):
        x_copy(h, 2).wait_recv()
        start(s_copy(h, 3))
        own_copy(h).wait()
        for n in range(4):
            s_copy(h, n).wait_recv()

    def c_copy(n, k):
        at = (x, x, jnp.where(core == 0, before, after))[k]
        target = (after, before, jnp.where(core == 0, after, before))[k]
        ref = panel[0].at[at, (z + NZ - n) % NZ, core]
        return send(ref, ref, c_sems, (n, k), to(target, z, core, y))

    def chunks(hop):
        if hop == 0:
            return [0]
        return [n for way, n in ((0, hop), (1, NZ - hop)) if hop <= z_hops[way]]

    def spread(hop):
        for n in chunks(hop):
            for k in range(2):
                start(c_copy(n, k))

    def relay(hop):
        for n in chunks(hop):
            for k in range(2):
                c_copy(n, k).wait_recv()
            start(c_copy(n, 2))

    def w_copy(n):
        at = (x, x, jnp.where(core == 0, before, after))[n]
        target = (after, before, jnp.where(core == 0, after, before))[n]
        return send(wide.at[at, z, core], wide.at[at, z, core], w_sems, (n,), to(target, z, core, y))

    def t_copy(n, slot):
        return send(wide.at[:, slot, core], wide.at[:, slot, core], t_sems, (n,), twin)

    def w_step(hop):
        z_step(1, hop)
        if hop == 0:
            start(t_copy(0, z))
        for way in range(2):
            if 1 <= hop <= z_hops[way]:
                start(t_copy(hop, (z + NZ - hop) % NZ) if way == 0 else t_copy(NZ - hop, (z + hop) % NZ))

    def w_end():
        for n in range(NZ):
            t_copy(n, z).wait_recv()

    greet(
        [to(after, z, core, y), to(before, z, core, y), to(x, west, core, y), to(x, east, core, y)]
        + [twin, to(x, z, core, south), to(x, z, core, north)]
    )

    at_row, at_lane = iota((TWO, TWO), 0), iota((TWO, TWO), 1)
    live = jnp.where(at_row < BLK, counts[0:1, 0:1], counts[1:2, 0:1])
    held = jnp.where((at_lane >= BLK).astype(I32) < live, tile[...], 0.0).T
    lane = iota((EXTRA, TWO), 1)
    mark = jnp.where(
        lane == 0,
        ids[0:1, 0:1],
        jnp.where(lane == 1, ids[0:1, 1:2], jnp.where(lane == 2, ids[1:2, 0:1], ids[1:2, 1:2])),
    ).astype(F32)
    row[y, :TWO] = held
    row[y, TWO:] = mark
    for h in range(NP):
        for s in range(2):
            chunk = held[s * BLK + AT[h] : s * BLK + AT[h] + WIDTHS[h]]
            if h == 0:
                panel[0][x, z, core, s * WIDTHS[0] : (s + 1) * WIDTHS[0]] = chunk
            elif h < AHEAD:
                at = sum(part_rows(g) for g in range(1, h)) + s * WIDTHS[h]
                early[z, at : at + WIDTHS[h]] = chunk
            else:
                at = ROWS[h] + s * WIDTHS[h]
                wide[x, z, core, at : at + WIDTHS[h]] = chunk
    panel[0][x, z, core, 2 * WIDTHS[0] :] = mark
    z_step(0, 0)
    spread(0)
    z_step(2, 0)
    r_step(0)
    for n in range(2):
        start(w_copy(n))

    first[8 * NY] = jnp.zeros((max(WIDTHS), TWO), F32)
    second[2 * per] = jnp.zeros((BLK, TWO), F32)
    square_iota = iota((per, per), 0) == iota((per, per), 1)
    keeps = [
        jnp.sum(jnp.where(square_iota, keep_pattern[r : r + 1, :], 0).astype(F32), axis=1, keepdims=True) for r in range(2)
    ]
    keep[...] = jnp.where(iota((per, TWO), 1) < BLK, keeps[0], keeps[1])

    for hop in range(1, max(NZ // 2, near) + 1):
        z_step(0, hop)
        spread(hop)
        if hop <= NZ // 2:
            relay(hop - 1)
        z_step(2, hop)
        r_step(hop)
        if hop == 1:
            for n in range(2):
                w_copy(n).wait_recv()
            start(w_copy(2))
        if hop == 2:
            w_copy(2).wait_recv()
            w_step(0)
        if hop == 4:
            w_step(1)
    start(s_copy(0, 0))
    relay(NZ // 2)
    for n in range(1, 3):
        start(s_copy(0, n))
    x_begin(1)
    w_step(2)
    for n in range(NZ):
        c_copy(n, 2).wait_recv()
    start(s_copy(0, 3))
    w_step(3)
    for n in range(4):
        s_copy(0, n).wait_recv()

    def tag_row(n, _):
        for c in range(2):
            tags[pl.ds(2 * n + c, 1), :] = panel[0][n // NZ, n % NZ, c, 2 * WIDTHS[0] : 2 * WIDTHS[0] + 1, :]
        return 0

    lax.fori_loop(0, NX * NZ, tag_row, 0)
    mine = jnp.concatenate([row[q, TWO : TWO + 1, :] for q in range(NY)], axis=0)
    for n, line in enumerate(make_tables(tags[...], mine, per)):
        table_v[n : n + 1, :] = line
    fetch = pltpu.make_async_copy(table_v, table, table_sem)
    fetch.start()
    fetch.wait()

    bits = NY.bit_length() - 1

    def block_of(h, along_x, along_z, side):
        return panel[min(h, AHEAD)][along_x, along_z, side, ROWS[h] : ROWS[h] + 2 * WIDTHS[h], :]

    def first_part(h):
        cp = WIDTHS[h]
        lanes = iota((2 * cp, TWO), 1) // BLK
        side = iota((cp, TWO), 1) // BLK

        def one_panel(q, _):
            high_w, low_w = split(row[q, :TWO])
            wide = jnp.concatenate([high_w, low_w], axis=1)
            stack = []
            for n in range(4):
                e = (n << bits) + q
                block = block_of(h, table[XS, e], table[ZS, e], table[CORES, e])
                block = jnp.where(table[HALF, e] == n % 2, block, pltpu.roll(block, BLK, 1))
                stack.append(jnp.where(lanes == n % 2, block, 0.0))
            high, low = split(jnp.concatenate(stack, axis=0))
            both = dot(high, wide)
            made = both[:, :TWO] + both[:, TWO:] + dot(low, high_w)
            for n in range(8):
                term = jnp.where(side == n // 4, made[n * cp : (n + 1) * cp], 0.0)
                first[q * 8 + n, :cp, :] = term + first[table[PREV1 + n % 2, ((n // 2) << bits) + q], :cp, :]
            return 0

        lax.fori_loop(0, NY, one_panel, 0)

        def one_column(j, _):
            parts[h][y, j] = first[table[LAST1, j], :cp, :] * keep[pl.ds(j, 1), :]
            return 0

        lax.fori_loop(0, per, one_column, 0)

    def second_pass(q, fresh):
        def one_device(d, _):
            device = q * (per // 2) + d
            spot = (device // (2 * NZ), (device // 2) % NZ, device % 2)
            high, low = split(jnp.concatenate([block_of(h, *spot) for h in range(NP)], axis=0))
            none = jnp.zeros((BLK, TWO), BF16)
            upper, lower = [], []
            for r in range(2):
                pieces = split(jnp.concatenate([parts[h][q, d * 2 + r] for h in range(NP)], axis=0))
                for side, piece in zip((upper, lower), pieces):
                    side.append(jnp.concatenate([piece, none] if r == 0 else [none, piece], axis=1))
            made = dot(jnp.concatenate([high, low], axis=1), jnp.concatenate(upper + upper, axis=0))
            made = made + dot(high, jnp.concatenate(lower, axis=0))
            for r in range(2):
                for s in range(2):
                    term = jnp.concatenate(
                        [
                            made[2 * AT[h] + s * WIDTHS[h] : 2 * AT[h] + (s + 1) * WIDTHS[h], r * TWO : (r + 1) * TWO]
                            for h in range(NP)
                        ],
                        axis=0,
                    )
                    second[d * 4 + r * 2 + s] = term + second[table[PREV2 + r * 2 + s, device]]
            return 0

        lax.fori_loop(0, per // 2, one_device, 0)

        def one_column(j, _):
            at = q * per + j
            new = second[table[LAST2 + at // TWO, at % TWO]]
            total[j] = new if fresh else total[j] + new
            return 0

        lax.fori_loop(0, per, one_column, 0)

    def own(pair):
        return jnp.concatenate([parts[h][y, pair * 2 + b] for b in range(2) for h in range(NP)], axis=0)

    def arrive(*steps):
        for h, hop in steps:
            y_step(h, hop)

    def form(h):
        first_part(h)
        y_step(h, 0)

    def run(hop, way):
        if hop <= near and (way == 0 or 2 * hop < NY):
            second_pass((y + NY - hop) % NY if way == 0 else (y + hop) % NY, False)

    form(0)
    w_step(4)
    x_middle(1)
    w_step(5)
    arrive((0, 1))
    x_end(1)
    form(1)
    arrive((0, 2))
    for hop in range(6, NZ // 2 + 1):
        w_step(hop)
    w_end()
    form(2)
    arrive((1, 1))
    form(3)
    second_pass(y, True)
    arrive((0, 3), (2, 1), (1, 2), (3, 1))
    run(1, 1)
    arrive((0, 4), (2, 2))
    run(1, 0)
    arrive((1, 3), (3, 2))
    run(2, 1)
    arrive((2, 3))
    run(2, 0)
    arrive((1, 4), (3, 3))
    run(3, 1)
    arrive((2, 4))
    run(3, 0)
    for pair in range(per // 2):
        square[:, pair * TWO : (pair + 1) * TWO] = own(pair).T
    arrive((3, 4))
    run(4, 0)
    for pair in range(per // 2):
        cube = jnp.concatenate(
            [total[pair * 2 + b] * keep[pair * 2 + b : pair * 2 + b + 1, :] for b in range(2)], axis=0
        )
        purified[:, pair * TWO : (pair + 1) * TWO] = (3.0 * own(pair) - 2.0 * cube).T
    for c in started:
        c.wait_send()


def local(values, column_ids, counts, keep_pattern):
    per = keep_pattern.shape[1]
    ndev = NX * NZ * 2
    vmem = pl.BlockSpec(memory_space=pltpu.VMEM)

    def dma(*shape):
        return [pltpu.SemaphoreType.DMA(shape), pltpu.SemaphoreType.DMA(shape)]

    held = AHEAD + 1

    def body(ids, counts, tile, keep_pattern, square, purified, *rest):
        panel, parts, others, sems = rest[:held], rest[held : held + NP], rest[held + NP : held + NP + 9], rest[held + NP + 9 :]
        pairs = [sems[2 * n : 2 * n + 2] for n in range(8)]
        purify(
            per, ids, counts, tile, keep_pattern, square, purified, panel, parts, *others, *pairs, sems[16], sems[17]
        )

    out = jax.ShapeDtypeStruct((TWO, per * BLK), F32)
    return pl.pallas_call(
        body,
        out_shape=(out, out),
        in_specs=[vmem] * 4,
        out_specs=(vmem, vmem),
        scratch_shapes=[pltpu.VMEM((NX, NZ, 2, part_rows(h), TWO), F32) for h in range(AHEAD)]
        + [pltpu.VMEM((NX, NZ, 2, sum(part_rows(h) for h in range(AHEAD, NP)), TWO), F32)]
        + [pltpu.VMEM((NY, per, WIDTHS[h], TWO), F32) for h in range(NP)]
        + [
            pltpu.VMEM((NY, TWO + EXTRA, TWO), F32),
            pltpu.VMEM((NZ, sum(part_rows(h) for h in range(1, AHEAD)), TWO), F32),
            pltpu.VMEM((8 * NY + 1, max(WIDTHS), TWO), F32),
            pltpu.VMEM((2 * per + 1, BLK, TWO), F32),
            pltpu.VMEM((per, BLK, TWO), F32),
            pltpu.VMEM((per, TWO), F32),
            pltpu.VMEM((ndev, TWO), F32),
            pltpu.VMEM((TABLE, TWO), I32),
            pltpu.SMEM((TABLE, TWO), I32),
        ]
        + dma(3, 2, NZ) + dma(2, NY) + dma(AHEAD, 3) + dma(AHEAD, 4) + dma(NP, 2, NY) + dma(3) + dma(NZ) + dma(NZ, 3)
        + [pltpu.SemaphoreType.DMA((AHEAD,)), pltpu.SemaphoreType.DMA],
        compiler_params=pltpu.CompilerParams(collective_id=0, has_side_effects=True, vmem_limit_bytes=48 << 20),
        name="purify",
    )(column_ids, counts, values, keep_pattern)


def solution(mesh):
    return jax.shard_map(
        local,
        mesh=mesh,
        in_specs=(P("row", "col"), P("row", "col"), P("row", "col"), P("row", "col")),
        out_specs=(P("row", "col"), P("row", "col")),
        check_vma=False,
    )
```

```python
import jax
import jax.numpy as jnp
from jax import lax
from jax.experimental import pallas as pl
from jax.experimental.pallas import tpu as pltpu
from jax.sharding import PartitionSpec as P

MESH = pl.DeviceIdType.MESH
NX, NZ, NY = 4, 12, 8
BLK = 64
TWO = 2 * BLK
WIDTHS = (16, 16, 16, 16)
LONGER = (0, 1, 0, 1)
NP = len(WIDTHS)
AT = tuple(sum(WIDTHS[:h]) for h in range(NP))
AHEAD = 2
ROWS = tuple(2 * AT[h] - (2 * AT[AHEAD] if h >= AHEAD else 2 * AT[h]) for h in range(NP))
EXTRA = 8
F32, BF16, I32 = jnp.float32, jnp.bfloat16, jnp.int32


def place():
    row, col = lax.axis_index("row"), lax.axis_index("col")
    return row // (2 * NZ), (row // 2) % NZ, row % 2, col


def to(x, z, core, y):
    return ((x * NZ + z) * 2 + core, y)


def greet(partners):
    barrier = pltpu.get_barrier_semaphore()
    for partner in partners:
        pl.semaphore_signal(barrier, inc=1, device_id=partner, device_id_type=MESH)
    pl.semaphore_wait(barrier, len(partners))


def send(src, dst, sems, at, target):
    return pltpu.make_async_remote_copy(
        src_ref=src, dst_ref=dst, send_sem=sems[0].at[at], recv_sem=sems[1].at[at], device_id=target, device_id_type=MESH
    )


def split(a):
    high = a.astype(BF16)
    return high, (a - high.astype(F32)).astype(BF16)


def dot(a, b):
    return jnp.dot(a, b, preferred_element_type=F32)


def part_rows(h):
    return 2 * WIDTHS[h] + (EXTRA if h == 0 else 0)


def iota(shape, axis):
    return lax.broadcasted_iota(I32, shape, axis)


def over(a, size, count):
    return sum(((a >= size * n).astype(I32) for n in range(1, count)), jnp.zeros(a.shape, I32))


def make_tables(tags, mine, per):
    ndev = tags.shape[0]
    each = per // 2
    bits = NY.bit_length() - 1
    tags, mine = (jnp.clip(a.astype(I32), 0, per - 1) for a in (tags, mine))
    sub, lane = iota((ndev, TWO), 0), iota((ndev, TWO), 1)
    piece_s, piece_l = over(sub, each, NY), over(lane, each, NY + 1)
    ids = [jnp.broadcast_to(tags[:, n : n + 1], (ndev, TWO)) for n in range(4)]
    rank_s = [(sub - each * piece_s) * 4 + n for n in range(4)]

    def top(terms, none):
        best = None
        for mask, rank in terms:
            new = jnp.where(mask, rank, -1)
            best = new if best is None else jnp.maximum(best, new)
        best = jnp.max(best, axis=0, keepdims=True)
        return jnp.where(best < 0, none, best)

    lane1, sub1 = iota((NY, TWO), 1), iota((NY, TWO), 0)
    block = jnp.zeros((NY, TWO), I32)
    for n in range(4):
        hit = ((lane1 >> bits) == n) & ((lane1 & (NY - 1)) == sub1)
        block = block + jnp.where(hit, jnp.broadcast_to(mine[:, n : n + 1], (NY, TWO)), 0)
    block = jnp.sum(block, axis=0, keepdims=True)
    lane0 = iota((1, TWO), 1)
    half = block & 1
    device = (lane0 & (NY - 1)) * each + (block >> 1)
    onto = []
    for s in range(2):
        chosen = jnp.where(half == 0, ids[s], ids[2 + s])
        onto.append(jnp.sum(jnp.where(sub == device, chosen, 0), axis=0, keepdims=True))
    count = 4 * NY
    sub2, lane2 = iota((count, TWO), 0), iota((count, TWO), 1)
    onto_s = [
        jnp.broadcast_to(jnp.sum(jnp.where(sub2 == lane2, onto[s], 0), axis=1, keepdims=True), (count, TWO))
        for s in range(2)
    ]

    def rank1(a, s):
        return ((a & (NY - 1)) * 4 + (a >> bits)) * 2 + s

    along_x = over(device, 2 * NZ, NX)
    along_z = (device - 2 * NZ * along_x) >> 1
    rows = [along_x, half]
    for s in range(2):
        rows.append(
            top(
                (((onto_s[t] == onto[s]) & (rank1(sub2, t) < rank1(lane2, s)), rank1(sub2, t)) for t in range(2)), 8 * NY
            )
        )
    rows.append(top(((onto_s[t] == lane2, rank1(sub2, t)) for t in range(2)), 8 * NY))
    for n in range(4):
        own = jnp.sum(jnp.where(sub == lane, ids[n], 0), axis=0, keepdims=True)
        rank_l = (lane - each * piece_l) * 4 + n
        rows.append(
            top(
                (((piece_s == piece_l) & (ids[m] == own) & (rank_s[m] < rank_l), rank_s[m]) for m in range(4)), 2 * per
            )
        )
    for g in range(-(-NY * per // TWO)):
        where = lane + g * TWO
        q = over(where, per, NY + 1)
        column = where - per * q
        rows.append(top((((piece_s == q) & (ids[m] == column), rank_s[m]) for m in range(4)), 2 * per))
    blank = jnp.zeros((1, TWO), I32)
    rows = rows + [blank] * (ZS - len(rows)) + [along_z, device & 1]
    return rows + [blank] * (TABLE - len(rows))


XS, HALF, PREV1, LAST1, PREV2, LAST2, ZS, CORES, TABLE = 0, 1, 2, 4, 5, 9, 11, 12, 16


def purify(
    per, given, ids, counts, tile, keep_pattern, square, purified,
    panel, parts, row, early, first, second, total, keep, tags, table_v, table,
    z_sems, r_sems, x_sems, s_sems, y_sems, w_sems, t_sems, c_sems, own_sem, table_sem, load_sem,
):
    x, z, core, y = place()
    west, east = (z + NZ - 1) % NZ, (z + 1) % NZ
    south, north = (y + NY - 1) % NY, (y + 1) % NY
    before, after = (x + NX - 1) % NX, (x + 1) % NX
    twin = to(x, z, 1 - core, y)
    near = NY // 2
    wide = panel[AHEAD]
    z_hops = (NZ // 2, NZ - 1 - NZ // 2)
    r_hops = (near, NY - 1 - near)

    def y_hops(h):
        return r_hops if LONGER[h] == 0 else r_hops[::-1]

    started = []

    def start(c):
        c.start()
        started.append(c)

    def z_copy(g, way, hop):
        slot = (z + NZ - hop) % NZ if way == 0 else (z + hop) % NZ
        ref = (panel[0].at[x, slot, core], wide.at[:, slot, core], early.at[slot])[g]
        return send(ref, ref, z_sems, (g, way, hop), to(x, east if way == 0 else west, core, y))

    def z_step(g, hop):
        for way in range(2):
            if 1 <= hop <= z_hops[way]:
                z_copy(g, way, hop - 1).wait_recv()
            if hop < z_hops[way]:
                start(z_copy(g, way, hop))

    def ring_y(ref, sems, at, way, hop):
        slot = (y + NY - hop) % NY if way == 0 else (y + hop) % NY
        return send(ref.at[slot], ref.at[slot], sems, at + (way, hop), to(x, z, core, north if way == 0 else south))

    def r_step(hop):
        for way in range(2):
            if 1 <= hop <= r_hops[way]:
                ring_y(row, r_sems, (), way, hop - 1).wait_recv()
            if hop < r_hops[way]:
                start(ring_y(row, r_sems, (), way, hop))

    def y_step(h, hop):
        for way in range(2):
            if 1 <= hop <= y_hops(h)[way]:
                ring_y(parts[h], y_sems, (h,), way, hop - 1).wait_recv()
            if hop < y_hops(h)[way]:
                start(ring_y(parts[h], y_sems, (h,), way, hop))

    def slab(h, at):
        return panel[h].at[at, :, core]

    def source(h):
        at = sum(part_rows(g) for g in range(1, h))
        return early.at[:, at : at + part_rows(h)]

    def x_copy(h, n):
        if n == 0:
            return send(source(h), slab(h, x), x_sems, (h, 0), to(after, z, core, y))
        if n == 1:
            return send(source(h), slab(h, x), x_sems, (h, 1), to(before, z, core, y))
        held = slab(h, jnp.where(core == 0, before, after))
        return send(held, held, x_sems, (h, 2), to(jnp.where(core == 0, after, before), z, core, y))

    def own_copy(h):
        return pltpu.make_async_copy(source(h), slab(h, x), own_sem.at[h])

    def s_copy(h, n):
        if n == 0 and h > 0:
            return send(source(h), slab(h, x), s_sems, (h, 0), twin)
        held = slab(h, (x, before, after, (x + 2) % NX)[n])
        return send(held, held, s_sems, (h, n), twin)

    def x_begin(h):
        for n in range(2):
            start(x_copy(h, n))
        own_copy(h).start()
        start(s_copy(h, 0))

    def x_middle(h):
        for n in range(2):
            x_copy(h, n).wait_recv()
        start(x_copy(h, 2))
        for n in range(1, 3):
            start(s_copy(h, n))

    def x_end(h):
        x_copy(h, 2).wait_recv()
        start(s_copy(h, 3))
        own_copy(h).wait()
        for n in range(4):
            s_copy(h, n).wait_recv()

    def c_copy(n, k):
        at = (x, x, jnp.where(core == 0, before, after))[k]
        target = (after, before, jnp.where(core == 0, after, before))[k]
        ref = panel[0].at[at, (z + NZ - n) % NZ, core]
        return send(ref, ref, c_sems, (n, k), to(target, z, core, y))

    def chunks(hop):
        if hop == 0:
            return [0]
        return [n for way, n in ((0, hop), (1, NZ - hop)) if hop <= z_hops[way]]

    def spread(hop):
        for n in chunks(hop):
            for k in range(2):
                start(c_copy(n, k))

    def relay(hop):
        for n in chunks(hop):
            for k in range(2):
                c_copy(n, k).wait_recv()
            start(c_copy(n, 2))

    def w_copy(n):
        at = (x, x, jnp.where(core == 0, before, after))[n]
        target = (after, before, jnp.where(core == 0, after, before))[n]
        return send(wide.at[at, z, core], wide.at[at, z, core], w_sems, (n,), to(target, z, core, y))

    def t_copy(n, slot):
        return send(wide.at[:, slot, core], wide.at[:, slot, core], t_sems, (n,), twin)

    def w_step(hop):
        z_step(1, hop)
        if hop == 0:
            start(t_copy(0, z))
        for way in range(2):
            if 1 <= hop <= z_hops[way]:
                start(t_copy(hop, (z + NZ - hop) % NZ) if way == 0 else t_copy(NZ - hop, (z + hop) % NZ))

    def w_end():
        for n in range(NZ):
            t_copy(n, z).wait_recv()

    loads = [
        pltpu.make_async_copy(src, dst, load_sem.at[n])
        for n, (src, dst) in enumerate(zip(given, (ids, counts, tile, keep_pattern)))
    ]
    for load in loads:
        load.start()
    greet(
        [to(after, z, core, y), to(before, z, core, y), to(x, west, core, y), to(x, east, core, y)]
        + [twin, to(x, z, core, south), to(x, z, core, north)]
    )

    for load in loads:
        load.wait()
    at_row, at_lane = iota((TWO, TWO), 0), iota((TWO, TWO), 1)
    live = jnp.where(at_row < BLK, counts[0:1, 0:1], counts[0:1, 1:2])
    held = jnp.where((at_lane >= BLK).astype(I32) < live, tile[...], 0.0).T
    lane = iota((EXTRA, TWO), 1)
    mark = jnp.where(
        lane == 0,
        ids[0:1, 0:1],
        jnp.where(lane == 1, ids[0:1, 1:2], jnp.where(lane == 2, ids[1:2, 0:1], ids[1:2, 1:2])),
    ).astype(F32)
    row[y, :TWO] = held
    row[y, TWO:] = mark
    for h in range(NP):
        for s in range(2):
            chunk = held[s * BLK + AT[h] : s * BLK + AT[h] + WIDTHS[h]]
            if h == 0:
                panel[0][x, z, core, s * WIDTHS[0] : (s + 1) * WIDTHS[0]] = chunk
            elif h < AHEAD:
                at = sum(part_rows(g) for g in range(1, h)) + s * WIDTHS[h]
                early[z, at : at + WIDTHS[h]] = chunk
            else:
                at = ROWS[h] + s * WIDTHS[h]
                wide[x, z, core, at : at + WIDTHS[h]] = chunk
    panel[0][x, z, core, 2 * WIDTHS[0] :] = mark
    z_step(0, 0)
    spread(0)
    z_step(2, 0)
    r_step(0)
    for n in range(2):
        start(w_copy(n))

    first[8 * NY] = jnp.zeros((max(WIDTHS), TWO), F32)
    second[2 * per] = jnp.zeros((BLK, TWO), F32)
    square_iota = iota((per, per), 0) == iota((per, per), 1)
    keeps = [
        jnp.sum(jnp.where(square_iota, keep_pattern[r : r + 1, :], 0).astype(F32), axis=1, keepdims=True) for r in range(2)
    ]
    keep[...] = jnp.where(iota((per, TWO), 1) < BLK, keeps[0], keeps[1])

    for hop in range(1, max(NZ // 2, near) + 1):
        z_step(0, hop)
        spread(hop)
        if hop <= NZ // 2:
            relay(hop - 1)
        z_step(2, hop)
        r_step(hop)
        if hop == 1:
            for n in range(2):
                w_copy(n).wait_recv()
            start(w_copy(2))
        if hop == 2:
            w_copy(2).wait_recv()
            w_step(0)
        if hop == 4:
            w_step(1)
    start(s_copy(0, 0))
    relay(NZ // 2)
    for n in range(1, 3):
        start(s_copy(0, n))
    x_begin(1)
    w_step(2)
    for n in range(NZ):
        c_copy(n, 2).wait_recv()
    start(s_copy(0, 3))
    w_step(3)
    for n in range(4):
        s_copy(0, n).wait_recv()

    def tag_row(n, _):
        for c in range(2):
            tags[pl.ds(2 * n + c, 1), :] = panel[0][n // NZ, n % NZ, c, 2 * WIDTHS[0] : 2 * WIDTHS[0] + 1, :]
        return 0

    lax.fori_loop(0, NX * NZ, tag_row, 0)
    mine = jnp.concatenate([row[q, TWO : TWO + 1, :] for q in range(NY)], axis=0)
    for n, line in enumerate(make_tables(tags[...], mine, per)):
        table_v[n : n + 1, :] = line
    fetch = pltpu.make_async_copy(table_v, table, table_sem)
    fetch.start()
    fetch.wait()

    bits = NY.bit_length() - 1

    def block_of(h, along_x, along_z, side):
        return panel[min(h, AHEAD)][along_x, along_z, side, ROWS[h] : ROWS[h] + 2 * WIDTHS[h], :]

    def first_part(h):
        cp = WIDTHS[h]
        lanes = iota((2 * cp, TWO), 1) // BLK
        side = iota((cp, TWO), 1) // BLK

        def one_panel(q, _):
            high_w, low_w = split(row[q, :TWO])
            wide = jnp.concatenate([high_w, low_w], axis=1)
            stack = []
            for n in range(4):
                e = (n << bits) + q
                block = block_of(h, table[XS, e], table[ZS, e], table[CORES, e])
                block = jnp.where(table[HALF, e] == n % 2, block, pltpu.roll(block, BLK, 1))
                stack.append(jnp.where(lanes == n % 2, block, 0.0))
            high, low = split(jnp.concatenate(stack, axis=0))
            both = dot(high, wide)
            made = both[:, :TWO] + both[:, TWO:] + dot(low, high_w)
            for n in range(8):
                term = jnp.where(side == n // 4, made[n * cp : (n + 1) * cp], 0.0)
                first[q * 8 + n, :cp, :] = term + first[table[PREV1 + n % 2, ((n // 2) << bits) + q], :cp, :]
            return 0

        lax.fori_loop(0, NY, one_panel, 0)

        def one_column(j, _):
            parts[h][y, j] = first[table[LAST1, j], :cp, :] * keep[pl.ds(j, 1), :]
            return 0

        lax.fori_loop(0, per, one_column, 0)

    def second_pass(q, fresh):
        def one_device(d, _):
            device = q * (per // 2) + d
            spot = (device // (2 * NZ), (device // 2) % NZ, device % 2)
            high, low = split(jnp.concatenate([block_of(h, *spot) for h in range(NP)], axis=0))
            none = jnp.zeros((BLK, TWO), BF16)
            upper, lower = [], []
            for r in range(2):
                pieces = split(jnp.concatenate([parts[h][q, d * 2 + r] for h in range(NP)], axis=0))
                for side, piece in zip((upper, lower), pieces):
                    side.append(jnp.concatenate([piece, none] if r == 0 else [none, piece], axis=1))
            made = dot(jnp.concatenate([high, low], axis=1), jnp.concatenate(upper + upper, axis=0))
            made = made + dot(high, jnp.concatenate(lower, axis=0))
            for r in range(2):
                for s in range(2):
                    term = jnp.concatenate(
                        [
                            made[2 * AT[h] + s * WIDTHS[h] : 2 * AT[h] + (s + 1) * WIDTHS[h], r * TWO : (r + 1) * TWO]
                            for h in range(NP)
                        ],
                        axis=0,
                    )
                    second[d * 4 + r * 2 + s] = term + second[table[PREV2 + r * 2 + s, device]]
            return 0

        lax.fori_loop(0, per // 2, one_device, 0)

        def one_column(j, _):
            at = q * per + j
            new = second[table[LAST2 + at // TWO, at % TWO]]
            total[j] = new if fresh else total[j] + new
            return 0

        lax.fori_loop(0, per, one_column, 0)

    def own(pair):
        return jnp.concatenate([parts[h][y, pair * 2 + b] for b in range(2) for h in range(NP)], axis=0)

    def arrive(*steps):
        for h, hop in steps:
            y_step(h, hop)

    def form(h):
        first_part(h)
        y_step(h, 0)

    def run(hop, way):
        if hop <= near and (way == 0 or 2 * hop < NY):
            second_pass((y + NY - hop) % NY if way == 0 else (y + hop) % NY, False)

    form(0)
    w_step(4)
    x_middle(1)
    w_step(5)
    arrive((0, 1))
    x_end(1)
    form(1)
    arrive((0, 2))
    for hop in range(6, NZ // 2 + 1):
        w_step(hop)
    w_end()
    form(2)
    arrive((1, 1))
    form(3)
    second_pass(y, True)
    arrive((0, 3), (2, 1), (1, 2), (3, 1))
    run(1, 1)
    arrive((0, 4), (2, 2))
    run(1, 0)
    arrive((1, 3), (3, 2))
    run(2, 1)
    arrive((2, 3))
    run(2, 0)
    arrive((1, 4), (3, 3))
    run(3, 1)
    arrive((2, 4))
    run(3, 0)
    for pair in range(per // 2):
        square[:, pair * TWO : (pair + 1) * TWO] = own(pair).T
    arrive((3, 4))
    run(4, 0)
    for pair in range(per // 2):
        cube = jnp.concatenate(
            [total[pair * 2 + b] * keep[pair * 2 + b : pair * 2 + b + 1, :] for b in range(2)], axis=0
        )
        purified[:, pair * TWO : (pair + 1) * TWO] = (3.0 * own(pair) - 2.0 * cube).T
    for c in started:
        c.wait_send()


def local(values, column_ids, counts, keep_pattern):
    per = keep_pattern.shape[1]
    ndev = NX * NZ * 2
    vmem = pl.BlockSpec(memory_space=pltpu.VMEM)

    def dma(*shape):
        return [pltpu.SemaphoreType.DMA(shape), pltpu.SemaphoreType.DMA(shape)]

    held = AHEAD + 1

    inputs = (((2, 2), I32), ((1, 2), I32), ((TWO, TWO), F32), ((2, per), I32))

    def body(*refs):
        given, (square, purified), loaded, rest = refs[:4], refs[4:6], refs[6:10], refs[10:]
        panel, parts, others, sems = rest[:held], rest[held : held + NP], rest[held + NP : held + NP + 9], rest[held + NP + 9 :]
        pairs = [sems[2 * n : 2 * n + 2] for n in range(8)]
        purify(
            per, given, *loaded, square, purified, panel, parts, *others, *pairs, *sems[16:]
        )

    out = jax.ShapeDtypeStruct((TWO, per * BLK), F32)
    return pl.pallas_call(
        body,
        out_shape=(out, out),
        in_specs=[pl.BlockSpec(memory_space=pltpu.HBM)] * 4,
        out_specs=(vmem, vmem),
        scratch_shapes=[pltpu.VMEM(*shape) for shape in inputs]
        + [pltpu.VMEM((NX, NZ, 2, part_rows(h), TWO), F32) for h in range(AHEAD)]
        + [pltpu.VMEM((NX, NZ, 2, sum(part_rows(h) for h in range(AHEAD, NP)), TWO), F32)]
        + [pltpu.VMEM((NY, per, WIDTHS[h], TWO), F32) for h in range(NP)]
        + [
            pltpu.VMEM((NY, TWO + EXTRA, TWO), F32),
            pltpu.VMEM((NZ, sum(part_rows(h) for h in range(1, AHEAD)), TWO), F32),
            pltpu.VMEM((8 * NY + 1, max(WIDTHS), TWO), F32),
            pltpu.VMEM((2 * per + 1, BLK, TWO), F32),
            pltpu.VMEM((per, BLK, TWO), F32),
            pltpu.VMEM((per, TWO), F32),
            pltpu.VMEM((ndev, TWO), F32),
            pltpu.VMEM((TABLE, TWO), I32),
            pltpu.SMEM((TABLE, TWO), I32),
        ]
        + dma(3, 2, NZ) + dma(2, NY) + dma(AHEAD, 3) + dma(AHEAD, 4) + dma(NP, 2, NY) + dma(3) + dma(NZ) + dma(NZ, 3)
        + [pltpu.SemaphoreType.DMA((AHEAD,)), pltpu.SemaphoreType.DMA, pltpu.SemaphoreType.DMA((4,))],
        compiler_params=pltpu.CompilerParams(collective_id=0, has_side_effects=True, vmem_limit_bytes=63 << 20),
        name="purify",
    )(column_ids, counts.reshape(1, 2), values, keep_pattern)


def solution(mesh):
    return jax.shard_map(
        local,
        mesh=mesh,
        in_specs=(P("row", "col"), P("row", "col"), P("row", "col"), P("row", "col")),
        out_specs=(P("row", "col"), P("row", "col")),
        check_vma=False,
    )
```
